256 devices in a mesh: blk: 32 (over z_hi, x, y), dp: 8 (over z_lo, core).
Axes of the slice: x: 4, y: 4, z: 8 (z_hi: 2, z_lo: 4; z = z_hi * 4 + z_lo), core: 2. Of those that a mesh axis runs over, the one named last changes fastest.
Arguments:
- image_embed: bfloat16 [49152, 1024], P(('blk', 'dp')), may hold values from -0.19921875 to 0.19921875
- text_embed: bfloat16 [49152, 1024], P(('blk', 'dp')), may hold values from -0.19921875 to 0.19921875
- log_logit_scale: float32 [1], replicated, may hold values from 1.6 to 3
- logit_bias: float32 [1], replicated, may hold values from -7 to -5
Outputs:
- image_gradient: bfloat16 [49152, 1024], P(('blk', 'dp'))
- text_gradient: bfloat16 [49152, 1024], P(('blk', 'dp'))
- log_scale_gradient: float32 [1], replicated
- grad_bias: float32 [1], replicated
- loss: float32 [1], replicated
The draws below stay inside these ranges and needn't reach their ends.
All inputs are finite; a program needn't handle non-finite values.
Results may differ from the reference program's by a relative error of at most 0.001.
The reference program's roundings to bfloat16 on the way (of `coef_half`) count: a program that leaves them out, or rounds other values in their place, can miss the bound.
Values may be sent and summed in bfloat16 or wider, within the bound.
A program may use at most 128 MiB of HBM per device.

```python
import jax
import jax.numpy as jnp
from jax import lax

D = 1024
ROWS_DEV = 192
GROUP_ROWS = 6144
PAIR_BATCH = 49152
N_BLK = 32
N_DP = 8


def block_levels(stream_key, dims, shards, low, high):
    def one(dim, blocks):
        heights = jax.random.uniform(jax.random.fold_in(jax.random.fold_in(stream_key, 6), dim), (blocks,), jnp.float32, low / len(shards), high / len(shards))
        return jnp.repeat(jnp.exp(heights), dims[dim] // blocks).reshape((-1,) + (1,) * (len(dims) - dim - 1))

    gain = one(*shards[0])
    for cut in shards[1:]:
        gain = gain * one(*cut)
    return gain


def bell_draw(stream_key, shape, scale, limit, shards=(), kind=jnp.bfloat16):
    result = scale * jax.random.normal(stream_key, shape, jnp.float32)
    if shards:
        result = result * block_levels(stream_key, shape, shards, -0.22, 0.18)
    return jnp.clip(result, -limit, limit).astype(kind)


def setup_inputs(seed: int = 0) -> dict:
    arg_keys = jax.random.split(jax.random.key(seed), 5)
    return {
        "image_embed": bell_draw(arg_keys[0], (PAIR_BATCH, D), 0.03125, 0.19921875, ((0, 256),)),
        "text_embed": bell_draw(arg_keys[1], (PAIR_BATCH, D), 0.03125, 0.19921875, ((0, 256),)),
        "log_logit_scale": jnp.clip(jax.random.uniform(arg_keys[2], (1,), jnp.float32, 1.6, 3.0), 1.6, 3.0),
        "logit_bias": jnp.clip(jax.random.uniform(arg_keys[3], (1,), jnp.float32, -7.0, -5.0), -7.0, -5.0),
    }


EPS = 1e-06

def unit_rows(raw):
    widened = raw.astype(jnp.float32)
    inverse = lax.rsqrt(lax.optimization_barrier(jnp.sum(widened * widened, axis=1, keepdims=True)) + EPS)
    unit_vec = widened * inverse
    return (unit_vec, inverse, unit_vec.astype(jnp.bfloat16))

def to_groups(array):
    width = array.shape[-1]
    return array.reshape(N_BLK, N_DP, ROWS_DEV, width).transpose(1, 0, 2, 3).reshape(N_DP, GROUP_ROWS, width)

def gathered_groups(array):
    width = array.shape[-1]
    return array.reshape(N_DP, N_BLK, ROWS_DEV, width).transpose(1, 0, 2, 3).reshape(PAIR_BATCH, width)

def unscaled_gradient(unit_vec, inverse, scaled):
    along = lax.optimization_barrier(jnp.sum(unit_vec * scaled, axis=1, keepdims=True))
    return ((scaled - unit_vec * along) * inverse).astype(jnp.bfloat16)

def reference(image_embed, text_embed, log_logit_scale, logit_bias):
    logit_scale = jnp.exp(log_logit_scale[0])
    shift_bias = logit_bias[0]
    image_normalized_rows, image_inverse_norm, image_portion = unit_rows(image_embed)
    text_normalized_rows, text_inverse_norm, text_half = unit_rows(text_embed)

    def one_group(group_data):
        image_group, text_group = group_data
        cosine_matrix = jnp.dot(image_group, text_group.T, preferred_element_type=jnp.float32)
        logit_matrix = logit_scale * cosine_matrix + shift_bias
        row_ids = lax.broadcasted_iota(jnp.int32, cosine_matrix.shape, 0)
        col_ids = lax.broadcasted_iota(jnp.int32, cosine_matrix.shape, 1)
        pair_sign = jnp.where(row_ids == col_ids, 1.0, -1.0).astype(jnp.float32)
        pair_loss = jax.nn.softplus(-pair_sign * logit_matrix)
        pair_coef = -pair_sign * jax.nn.sigmoid(-pair_sign * logit_matrix)
        coef_half = pair_coef.astype(jnp.bfloat16)
        image_partial = jnp.dot(coef_half, text_group, preferred_element_type=jnp.float32)
        text_partial = jnp.dot(coef_half.T, image_group, preferred_element_type=jnp.float32)
        grand_totals = jnp.stack([jnp.sum(pair_loss), jnp.sum(pair_coef * cosine_matrix), jnp.sum(pair_coef)])
        return (image_partial, text_partial, grand_totals)
    image_partial, text_partial, grand_totals = lax.map(one_group, (to_groups(image_portion), to_groups(text_half)))
    image_gradient = unscaled_gradient(image_normalized_rows, image_inverse_norm, logit_scale * gathered_groups(image_partial))
    text_gradient = unscaled_gradient(text_normalized_rows, text_inverse_norm, logit_scale * gathered_groups(text_partial))
    reduced_sum = lax.optimization_barrier(jnp.sum(grand_totals, axis=0))
    loss = (reduced_sum[0] / PAIR_BATCH).reshape(1)
    log_scale_gradient = (logit_scale * reduced_sum[1] / PAIR_BATCH).reshape(1)
    grad_bias = (reduced_sum[2] / PAIR_BATCH).reshape(1)
    return (image_gradient, text_gradient, log_scale_gradient, grad_bias, loss)
```

```python
import functools

import jax
import jax.numpy as jnp
from jax import lax
from jax.experimental import pallas as pl
from jax.experimental.pallas import tpu as pltpu
from jax.sharding import PartitionSpec as P

EPS = 1e-06
MESH = pl.DeviceIdType.MESH
SIDE = 4
TILE = 256

Z_IN_T, Z_IN_I = 0, 1
AG_T, AG_I = 2, 5
CORE_T, CORE_I = 8, 12
RS_T, RS_I = 16, 19
Z_OUT_T, Z_OUT_I = 22, 23
ST_X, ST_Y, ST_C, ST_L, ST_P = 24, 27, 30, 31, 34
COPIES = 35


def kernel(
    pairs, log_scale_ref, bias_ref, img_ref, txt_ref,
    out_img, out_txt, out_scale, out_bias, out_loss,
    raw, texts, images, coef_own, coef_other, grad_img, grad_txt, recv_img, recv_txt,
    final, acc, st_x, st_y, st_c, st_l, st_p, send_sem, recv_sem,
):
    rows, width = img_ref.shape
    half = SIDE * rows
    blk, dp = lax.axis_index("blk"), lax.axis_index("dp")
    zh, x, y = blk // (SIDE * SIDE), (blk // SIDE) % SIDE, blk % SIDE
    zl, core = dp // 2, dp % 2
    native = core == zh

    def device(dx=0, dy=0, dl=0, other_core=False, other_plane=False):
        h = 1 - zh if other_plane else zh
        c = 1 - core if other_core else core
        return {
            "blk": (h * SIDE + (x + dx) % SIDE) * SIDE + (y + dy) % SIDE,
            "dp": ((zl + dl) % SIDE) * 2 + c,
        }

    along_x = [device(dx=d) for d in (1, 2, 3)]
    along_y = [device(dy=d) for d in (1, 2, 3)]
    along_l = [device(dl=d) for d in (1, 2, 3)]
    sibling = device(other_core=True)
    partner = device(other_core=True, other_plane=True)

    def copy(number, src, dst, where):
        return pltpu.make_async_remote_copy(
            src_ref=src, dst_ref=dst, send_sem=send_sem.at[number], recv_sem=recv_sem.at[number],
            device_id=where, device_id_type=MESH,
        )

    def slot(buffer, index):
        return buffer.at[pl.ds(index * rows, rows)]

    def z_in(number):
        src = (txt_ref, img_ref)[number - Z_IN_T]
        return copy(number, src, raw.at[number - Z_IN_T], partner)

    def gather(base, d):
        buffer, line = (texts, along_x) if base == AG_T else (images, along_y)
        return copy(base + d - 1, slot(buffer, 0), slot(buffer, SIDE - d), line[d - 1])

    def to_core(base, index):
        buffer = texts if base == CORE_T else images
        return copy(base + index, slot(buffer, index), slot(buffer, SIDE + index), sibling)

    def reduce(base, d):
        grad, recv, line = (grad_txt, recv_txt, along_x) if base == RS_T else (grad_img, recv_img, along_y)
        return copy(base + d - 1, slot(grad, d), recv.at[d - 1], line[d - 1])

    def z_out(number):
        which = number - Z_OUT_T
        return copy(number, final.at[which], (out_txt, out_img)[which], partner)

    barrier = pltpu.get_barrier_semaphore()
    everyone = along_x + along_y + along_l + [sibling, partner]
    for other in everyone:
        pl.semaphore_signal(barrier, inc=1, device_id=other, device_id_type=MESH)
    pl.semaphore_wait(barrier, len(everyone))

    def normalize(which, buffer):
        def body(i, _):
            at = pl.ds(pl.multiple_of(i * 16, 16), 16)
            wide = raw[which, at, :].astype(jnp.float32)
            inverse = lax.rsqrt(jnp.sum(wide * wide, axis=1, keepdims=True) + EPS)
            buffer[at, :] = (wide * inverse).astype(jnp.bfloat16)
            return 0

        lax.fori_loop(0, rows // 16, body, 0)

    def share(which, buffer, ag, to):
        normalize(which, buffer)
        for d in (1, 3, 2):
            gather(ag, d).start()
        to_core(to, 0).start()

    def forward(ag, to):
        for d in (1, 3, 2):
            gather(ag, d).wait_recv()
            to_core(to, SIDE - d).start()

    acc[...] = jnp.zeros_like(acc)

    @pl.when(jnp.logical_not(native))
    def _():
        z_in(Z_IN_T).start()
        z_in(Z_IN_I).start()
        z_in(Z_IN_T).wait_recv()

    @pl.when(native)
    def _():
        raw[0] = txt_ref[...]
        raw[1] = img_ref[...]

    scale = jnp.exp(jnp.full((1, TILE), log_scale_ref[0], jnp.float32))
    bias = jnp.full((1, TILE), bias_ref[0], jnp.float32)

    share(0, texts, AG_T, CORE_T)

    @pl.when(native)
    def _():
        share(1, images, AG_I, CORE_I)

    forward(AG_T, CORE_T)
    for index in range(SIDE):
        to_core(CORE_T, index).wait_recv()

    def cosines(left, right):
        return lax.dot_general(left, right, (((1,), (1,)), ((), ())), preferred_element_type=jnp.float32)

    def other_part():
        for index in range(SIDE):
            to_core(CORE_I, index).wait_recv()
        tiles = half // TILE

        def body(step, _):
            i, j = step // tiles, step % tiles
            left = images[pl.ds(pl.multiple_of(half + i * TILE, TILE), TILE), :]
            right = texts[pl.ds(pl.multiple_of(j * TILE, TILE), TILE), :]
            grown = jnp.exp(scale * cosines(left, right) + bias)
            coef_other[pl.ds(pl.multiple_of(i * TILE, TILE), TILE), pl.ds(pl.multiple_of(j * TILE, TILE), TILE)] = (
                grown / (1.0 + grown)
            ).astype(jnp.bfloat16)
            return 0

        lax.fori_loop(0, tiles * tiles, body, 0)

    @pl.when(jnp.logical_not(native))
    def _():
        other_part()
        z_in(Z_IN_I).wait_recv()
        share(1, images, AG_I, CORE_I)

    def own_tile(index, j, diagonal):
        left = images[pl.ds(index * rows, rows), :]
        right = texts[pl.ds(pl.multiple_of(j * TILE, TILE), TILE), :]
        cosine = cosines(left, right)
        logit = scale * cosine + bias
        grown = jnp.exp(logit)
        more = 1.0 + grown
        inverse = 1.0 / more
        coef = grown * inverse
        loss = jnp.log(more)
        if diagonal:
            same = lax.broadcasted_iota(jnp.int32, cosine.shape, 0) == lax.broadcasted_iota(jnp.int32, cosine.shape, 1)
            coef = jnp.where(same, -inverse, coef)
            loss = jnp.where(same, loss - logit, loss)
        coef_own[pl.ds(index * rows, rows), pl.ds(pl.multiple_of(j * TILE, TILE), TILE)] = coef.astype(jnp.bfloat16)
        for k, term in enumerate((loss, coef * cosine, coef)):
            acc[k] += jnp.sum(term.reshape(rows // 8, 8, TILE), axis=0)

    def image_slot(index):
        start = 0
        if index == 0:
            own_tile(0, 0, True)
            start = 1

        def tile(j, _):
            own_tile(index, j, False)
            return 0

        lax.fori_loop(start, 2 * half // TILE, tile, 0)

        def column(n, _):
            at = pl.ds(pl.multiple_of(n * TILE, TILE), TILE)
            grad_img[pl.ds(index * rows, rows), at] = jnp.dot(
                coef_own[pl.ds(index * rows, rows), :], texts[:, at], preferred_element_type=jnp.float32
            )
            return 0

        lax.fori_loop(0, width // TILE, column, 0)

    image_slot(0)
    for d in (1, 3, 2):
        gather(AG_I, d).wait_recv()
        to_core(CORE_I, SIDE - d).start()
        image_slot(SIDE - d)
        reduce(RS_I, SIDE - d).start()

    @pl.when(native)
    def _():
        other_part()

    def sums_start(base, buffer, mine, line):
        for d in range(1, len(line) + 1):
            copy(base + d - 1, buffer.at[mine], buffer.at[mine], line[d - 1]).start()

    def sums_finish(base, buffer, mine, line):
        for d in range(1, len(line) + 1):
            copy(base + d - 1, buffer.at[mine], buffer.at[mine], line[d - 1]).wait_recv()
        return functools.reduce(lambda a, b: a + b, [buffer[i] for i in range(len(line) + 1)])

    stages = (
        (ST_X, st_x, x, along_x),
        (ST_Y, st_y, y, along_y),
        (ST_C, st_c, core, [sibling]),
        (ST_L, st_l, zl, along_l),
        (ST_P, st_p, zh, [partner]),
    )
    folded = acc[:, :, :128] + acc[:, :, 128:]
    st_x[x] = folded.reshape(24, 128)
    sums_start(*stages[0])

    def text_tile(jt):
        at_rows = pl.ds(jt * TILE, TILE)

        def column(n, _):
            at = pl.ds(pl.multiple_of(n * TILE, TILE), TILE)
            over_rows = (((0,), (0,)), ((), ()))
            grad_txt[at_rows, at] = lax.dot_general(
                coef_own[:, at_rows], images[:half, at], over_rows, preferred_element_type=jnp.float32
            ) + lax.dot_general(
                coef_other[:, at_rows], images[half:, at], over_rows, preferred_element_type=jnp.float32
            )
            return 0

        lax.fori_loop(0, width // TILE, column, 0)

    text_tile(1)
    text_tile(2)
    reduce(RS_T, 2).start()
    reduce(RS_T, 3).start()
    text_tile(0)
    reduce(RS_T, 1).start()

    for this, after in zip(stages[:-1], stages[1:]):
        after[1][after[2]] = sums_finish(*this)
        sums_start(*after)
    totals = sums_finish(*stages[-1])
    loss_sum, temp_sum, bias_sum = (
        jnp.sum(jnp.sum(totals[8 * k : 8 * k + 8], axis=0, keepdims=True), axis=1, keepdims=True) for k in range(3)
    )
    out_loss[0] = (loss_sum / pairs)[0, 0]
    out_scale[0] = (scale[:, :1] * temp_sum / pairs)[0, 0]
    out_bias[0] = (bias_sum / pairs)[0, 0]

    def finish(which, grad, recv):
        def body(i, _):
            at = pl.ds(pl.multiple_of(i * 16, 16), 16)
            wide = raw[which, at, :].astype(jnp.float32)
            inverse = lax.rsqrt(jnp.sum(wide * wide, axis=1, keepdims=True) + EPS)
            unit = wide * inverse
            scaled = scale[:, :1] * (grad[at, :] + recv[0, at, :] + recv[1, at, :] + recv[2, at, :])
            along = jnp.sum(unit * scaled, axis=1, keepdims=True)
            final[which, at, :] = ((scaled - unit * along) * inverse).astype(jnp.bfloat16)
            return 0

        lax.fori_loop(0, rows // 16, body, 0)

    for which, rs, grad, recv, out, number in (
        (1, RS_I, grad_img, recv_img, out_img, Z_OUT_I),
        (0, RS_T, grad_txt, recv_txt, out_txt, Z_OUT_T),
    ):
        for d in (1, 2, 3):
            reduce(rs, d).wait_recv()
        finish(which, grad, recv)

        @pl.when(native)
        def _():
            out[...] = final[which]

        @pl.when(jnp.logical_not(native))
        def _():
            z_out(number).start()

    for d in (1, 2, 3):
        gather(AG_T, d).wait_send()
        gather(AG_I, d).wait_send()
        reduce(RS_T, d).wait_send()
        reduce(RS_I, d).wait_send()
    for index in range(SIDE):
        to_core(CORE_T, index).wait_send()
        to_core(CORE_I, index).wait_send()
    for base, buffer, mine, line in stages:
        for d in range(1, len(line) + 1):
            copy(base + d - 1, buffer.at[mine], buffer.at[mine], line[d - 1]).wait_send()

    @pl.when(jnp.logical_not(native))
    def _():
        z_in(Z_IN_T).wait_send()
        z_in(Z_IN_I).wait_send()
        z_out(Z_OUT_I).wait()
        z_out(Z_OUT_T).wait()


def per_device(image_embed, text_embed, log_logit_scale, logit_bias):
    rows, width = image_embed.shape
    half = SIDE * rows
    pairs = rows * lax.axis_size("blk") * lax.axis_size("dp")
    vmem, smem = pl.BlockSpec(memory_space=pltpu.VMEM), pl.BlockSpec(memory_space=pltpu.SMEM)
    one = jax.ShapeDtypeStruct((1,), jnp.float32)
    like = jax.ShapeDtypeStruct((rows, width), jnp.bfloat16)
    bf16, f32 = jnp.bfloat16, jnp.float32
    image_gradient, text_gradient, scale_gradient, bias_gradient, loss = pl.pallas_call(
        functools.partial(kernel, pairs),
        out_shape=(like, like, one, one, one),
        in_specs=[smem, smem, vmem, vmem],
        out_specs=(vmem, vmem, smem, smem, smem),
        scratch_shapes=[
            pltpu.VMEM((2, rows, width), bf16),
            pltpu.VMEM((2 * half, width), bf16),
            pltpu.VMEM((2 * half, width), bf16),
            pltpu.VMEM((half, 2 * half), bf16),
            pltpu.VMEM((half, half), bf16),
            pltpu.VMEM((half, width), f32),
            pltpu.VMEM((half, width), f32),
            pltpu.VMEM((3, rows, width), f32),
            pltpu.VMEM((3, rows, width), f32),
            pltpu.VMEM((2, rows, width), bf16),
            pltpu.VMEM((3, 8, TILE), f32),
            pltpu.VMEM((4, 24, 128), f32),
            pltpu.VMEM((4, 24, 128), f32),
            pltpu.VMEM((2, 24, 128), f32),
            pltpu.VMEM((4, 24, 128), f32),
            pltpu.VMEM((2, 24, 128), f32),
            pltpu.SemaphoreType.DMA((COPIES,)),
            pltpu.SemaphoreType.DMA((COPIES,)),
        ],
        name="contrastive_step",
        compiler_params=pltpu.CompilerParams(
            collective_id=0, has_side_effects=True, vmem_limit_bytes=48 * 2**20
        ),
    )(log_logit_scale, logit_bias, image_embed, text_embed)
    return image_gradient, text_gradient, scale_gradient, bias_gradient, loss


def solution(mesh):
    placed = (P(("blk", "dp"), None), P(("blk", "dp"), None), P(), P())
    return jax.shard_map(
        per_device,
        mesh=mesh,
        in_specs=placed,
        out_specs=(P(("blk", "dp"), None), P(("blk", "dp"), None), P(), P(), P()),
        check_vma=False,
    )
```

```python
import functools

import jax
import jax.numpy as jnp
from jax import lax
from jax.experimental import pallas as pl
from jax.experimental.pallas import tpu as pltpu
from jax.sharding import PartitionSpec as P

EPS = 1e-06
LOG2E = 1.4426950408889634
LN2 = 0.6931471805599453
MESH = pl.DeviceIdType.MESH
SIDE = 4
TILE = 256
TXT, IMG = 0, 1
A, B = 0, 1
OVER_COLS = (((1,), (1,)), ((), ()))
OVER_ROWS = (((0,), (0,)), ((), ()))

Z_IN, GATHER, RELAY, CORE, REDUCE, Z_OUT = 0, 4, 12, 16, 32, 44
ST_X, ST_Y, ST_C, ST_L, ST_P = 48, 51, 54, 55, 58
COPIES = 59


def kernel(
    pairs, log_scale_ref, bias_ref, img_ref, txt_ref,
    out_img, out_txt, out_scale, out_bias, out_loss,
    raw, inverses, texts, images, coef_own, coef_other, cos_even, cos_odd,
    grad_txt, grad_img, recv_txt, recv_img, relay_txt, relay_img,
    final, acc, st_x, st_y, st_c, st_l, st_p, send_sem, recv_sem, local_sem,
):
    rows, width = img_ref.shape
    part = rows // 2
    block = SIDE * part
    share = 2 * block
    blk, dp = lax.axis_index("blk"), lax.axis_index("dp")
    zh, x, y = blk // (SIDE * SIDE), (blk // SIDE) % SIDE, blk % SIDE
    zl, core = dp // 2, dp % 2
    native = core == zh

    def device(dx=0, dy=0, dl=0, other_core=False, other_plane=False):
        h = 1 - zh if other_plane else zh
        c = 1 - core if other_core else core
        return {
            "blk": (h * SIDE + (x + dx) % SIDE) * SIDE + (y + dy) % SIDE,
            "dp": ((zl + dl) % SIDE) * 2 + c,
        }

    along_x = [device(dx=d) for d in (1, 2, 3)]
    along_y = [device(dy=d) for d in (1, 2, 3)]
    along_l = [device(dl=d) for d in (1, 2, 3)]
    right = (along_x[0], along_y[0])
    left = (along_x[2], along_y[2])
    sibling = device(other_core=True)
    partner = device(other_core=True, other_plane=True)
    inputs, outputs = (txt_ref, img_ref), (out_txt, out_img)
    units, grads = (texts, images), (grad_txt, grad_img)
    recvs, relays = (recv_txt, recv_img), (relay_txt, relay_img)

    def copy(number, src, dst, where):
        return pltpu.make_async_remote_copy(
            src_ref=src, dst_ref=dst, send_sem=send_sem.at[number], recv_sem=recv_sem.at[number],
            device_id=where, device_id_type=MESH,
        )

    def half(h):
        return pl.ds(h * part, part)

    def slot(h, index, other=0):
        return pl.ds(other * share + h * block + index * part, part)

    def z_in(t, h):
        return copy(Z_IN + 2 * t + h, inputs[t].at[half(h)], raw.at[t, half(h)], partner)

    def gather(t, h, d):
        return copy(
            GATHER + 4 * t + 2 * h + d, units[t].at[slot(h, 0)], units[t].at[slot(h, (3, 1)[d])], (right, left)[d][t]
        )

    def relay(t, h):
        return copy(
            RELAY + 2 * t + h, units[t].at[slot(h, (3, 1)[h])], units[t].at[slot(h, 2)], (right, left)[h][t]
        )

    def to_core(t, h, index):
        return copy(
            CORE + 8 * t + 4 * h + index, units[t].at[slot(h, index)], units[t].at[slot(h, index, 1)], sibling
        )

    def reduce(t, h, step):
        onward = step != 1
        to = (right, left)[h if onward else 1 - h][t]
        if step == 0:
            src, dst = slot(h, 2), relays[t].at[h]
        elif step == 1:
            src, dst = slot(h, (3, 1)[h]), recvs[t].at[1 - h, half(h)]
        else:
            src, dst = slot(h, (1, 3)[h]), recvs[t].at[h, half(h)]
        return copy(REDUCE + 6 * t + 3 * h + step, grads[t].at[src], dst, to)

    def z_out(t, h):
        return copy(Z_OUT + 2 * t + h, final.at[t, half(h)], outputs[t].at[half(h)], partner)

    def local_in(t):
        return pltpu.make_async_copy(inputs[t], raw.at[t], local_sem.at[t])

    def local_out(t, h):
        return pltpu.make_async_copy(final.at[t, half(h)], outputs[t].at[half(h)], local_sem.at[2 + 2 * t + h])

    @pl.when(native)
    def _():
        local_in(TXT).start()
        local_in(IMG).start()

    barrier = pltpu.get_barrier_semaphore()
    everyone = along_x + along_y + along_l + [sibling, partner]
    for other in everyone:
        pl.semaphore_signal(barrier, inc=1, device_id=other, device_id_type=MESH)
    pl.semaphore_wait(barrier, len(everyone))

    log_scale = jnp.full((1, TILE), log_scale_ref[0], jnp.float32)
    scale = jnp.exp(log_scale)
    scale2 = scale * LOG2E
    bias2 = jnp.full((1, TILE), bias_ref[0], jnp.float32) * LOG2E
    acc[...] = jnp.zeros_like(acc)

    def normalize(t, h):
        for i in range(part // 32):
            at = pl.ds(h * part + i * 32, 32)
            wide = raw[t, at, :].astype(jnp.float32)
            inverse = lax.rsqrt(jnp.sum(wide * wide, axis=1, keepdims=True) + EPS)
            inverses[t, at, :] = jnp.broadcast_to(inverse, (32, 128))
            units[t][pl.ds(h * block + i * 32, 32), :] = (wide * inverse).astype(jnp.bfloat16)

    def send_half(t, h):
        normalize(t, h)
        gather(t, h, h).start()
        gather(t, h, 1 - h).start()
        to_core(t, h, 0).start()

    def pass_on(t, h):
        gather(t, h, h).wait_recv()
        relay(t, h).start()
        to_core(t, h, (3, 1)[h]).start()
        gather(t, h, 1 - h).wait_recv()
        to_core(t, h, (1, 3)[h]).start()

    def pass_last(t, h):
        relay(t, h).wait_recv()
        to_core(t, h, 2).start()

    def from_core(t, h):
        for index in range(SIDE):
            to_core(t, h, index).wait_recv()

    def dot_tile(out, first, column):
        out[...] = lax.dot_general(
            images[pl.ds(first, block), :],
            texts[pl.ds(pl.multiple_of(column * TILE, TILE), TILE), :],
            OVER_COLS,
            preferred_element_type=jnp.float32,
        )

    def own_terms(cos_ref, h, column):
        at_cols = pl.ds(pl.multiple_of(column * TILE, TILE), TILE)
        losses = temps = biases = jnp.zeros((8, TILE), jnp.float32)
        strip = 16
        for i in range(block // strip):
            cosine = cos_ref[pl.ds(i * strip, strip), :]
            grown = jnp.exp2(scale2 * cosine + bias2)
            more = 1.0 + grown
            coef = grown / more
            coef_own[pl.ds(h * block + i * strip, strip), at_cols] = coef.astype(jnp.bfloat16)
            fold = (strip // 8, 8, TILE)
            losses += jnp.sum(jnp.log(more).reshape(fold), axis=0)
            temps += jnp.sum((coef * cosine).reshape(fold), axis=0)
            biases += jnp.sum(coef.reshape(fold), axis=0)
        acc[0] += losses
        acc[1] += temps
        acc[2] += biases

    def other_terms(cos_ref, h, column):
        at_cols = pl.ds(pl.multiple_of(column * TILE, TILE), TILE)
        strip = 16
        for i in range(block // strip):
            grown = jnp.exp2(scale2 * cos_ref[pl.ds(i * strip, strip), :] + bias2)
            coef_other[pl.ds(h * block + i * strip, strip), at_cols] = (grown / (1.0 + grown)).astype(jnp.bfloat16)

    def sweep(terms, first, h, start, stop):
        dot_tile(cos_even, first, start)
        count = stop - start

        def body(p, _):
            column = start + 2 * p
            dot_tile(cos_odd, first, column + 1)
            terms(cos_even, h, column)
            dot_tile(cos_even, first, jnp.minimum(column + 2, stop - 1))
            terms(cos_odd, h, column + 1)
            return 0

        lax.fori_loop(0, count // 2, body, 0)
        if count % 2:
            terms(cos_even, h, stop - 1)

    def own_logits(h, start, stop):
        sweep(own_terms, h * block, h, start, stop)

    def other_logits(h):
        sweep(other_terms, share + h * block, h, 0, share // TILE)

    def same_pairs(h):
        lanes = 128
        at_rows, at_cols = pl.ds(h * block, part), pl.ds(h * block, lanes)
        cosine = lax.dot_general(
            images[at_rows, :], texts[at_cols, :], OVER_COLS, preferred_element_type=jnp.float32
        )
        shape = (part, lanes)
        same = lax.broadcasted_iota(jnp.int32, shape, 0) == lax.broadcasted_iota(jnp.int32, shape, 1)
        grown = jnp.exp2(scale2[:, :lanes] * cosine + bias2[:, :lanes])
        more = 1.0 + grown
        inverse = 1.0 / more
        coef = grown * inverse
        coef_own[at_rows, at_cols] = jnp.where(same, -inverse, coef).astype(jnp.bfloat16)
        logit = scale[:, :lanes] * cosine + bias_ref[0]
        change = jnp.where(same, -inverse - coef, 0.0)
        fold = (part // 8, 8, lanes)
        acc[0, :, :lanes] += jnp.sum(jnp.where(same, -logit, 0.0).reshape(fold), axis=0)
        acc[1, :, :lanes] += jnp.sum((change * cosine).reshape(fold), axis=0)
        acc[2, :, :lanes] += jnp.sum(change.reshape(fold), axis=0)

    def image_terms(h):
        def column(n, _):
            at = pl.ds(pl.multiple_of(n * TILE, TILE), TILE)
            grad_img[pl.ds(h * block, block), at] = jnp.dot(
                coef_own[pl.ds(h * block, block), :], texts[:, at], preferred_element_type=jnp.float32
            )
            return 0

        lax.fori_loop(0, width // TILE, column, 0)
        reduce(IMG, h, 0).start()
        reduce(IMG, h, 1).start()

    def text_terms(h):
        at_rows = pl.ds(h * block, block)

        def column(n, _):
            at = pl.ds(pl.multiple_of(n * TILE, TILE), TILE)
            grad_txt[at_rows, at] = lax.dot_general(
                coef_own[:, at_rows], images[:share, at], OVER_ROWS, preferred_element_type=jnp.float32
            ) + lax.dot_general(
                coef_other[:, at_rows], images[share:, at], OVER_ROWS, preferred_element_type=jnp.float32
            )
            return 0

        lax.fori_loop(0, width // TILE, column, 0)
        reduce(TXT, h, 0).start()
        reduce(TXT, h, 1).start()

    def add_relayed(t, h):
        reduce(t, h, 0).wait_recv()
        grads[t][slot(h, (1, 3)[h]), :] += relays[t][h]
        reduce(t, h, 2).start()

    def finish(t, h):
        reduce(t, h, 1).wait_recv()
        reduce(t, h, 2).wait_recv()
        for i in range(part // 16):
            at = pl.ds(h * part + i * 16, 16)
            inverse = inverses[t, at, :1]
            unit = raw[t, at, :].astype(jnp.float32) * inverse
            scaled = scale[:, :1] * (
                grads[t][pl.ds(h * block + i * 16, 16), :] + recvs[t][0, at, :] + recvs[t][1, at, :]
            )
            along = jnp.sum(unit * scaled, axis=1, keepdims=True)
            final[t, at, :] = ((scaled - unit * along) * inverse).astype(jnp.bfloat16)

    stages = (
        (ST_X, st_x, x, along_x),
        (ST_Y, st_y, y, along_y),
        (ST_C, st_c, core, [sibling]),
        (ST_L, st_l, zl, along_l),
        (ST_P, st_p, zh, [partner]),
    )

    def stage_copies(base, buffer, mine, line):
        return [copy(base + i, buffer.at[mine], buffer.at[mine], other) for i, other in enumerate(line)]

    def sums_start(stage, value):
        _, buffer, mine, _ = stages[stage]
        buffer[mine] = value
        for each in stage_copies(*stages[stage]):
            each.start()

    def sums_finish(stage):
        for each in stage_copies(*stages[stage]):
            each.wait_recv()
        buffer, count = stages[stage][1], len(stages[stage][3]) + 1
        return functools.reduce(lambda a, b: a + b, [buffer[i] for i in range(count)])

    def sums_first():
        sums_start(0, (acc[:, :, :128] + acc[:, :, 128:]).reshape(24, 128))

    def sums_next(stage):
        sums_start(stage, sums_finish(stage - 1))

    def sums_last():
        totals = sums_finish(len(stages) - 1)
        loss_sum, temp_sum, bias_sum = (
            jnp.sum(jnp.sum(totals[8 * k : 8 * k + 8], axis=0, keepdims=True), axis=1, keepdims=True)
            for k in range(3)
        )
        out_loss[0] = (loss_sum / pairs)[0, 0]
        out_scale[0] = (scale[:, :1] * temp_sum / pairs)[0, 0]
        out_bias[0] = (bias_sum / pairs)[0, 0]

    tiles = share // TILE

    @pl.when(native)
    def _():
        for t in (TXT, IMG):
            local_in(t).wait()
            send_half(t, A)
            send_half(t, B)
        for t in (TXT, IMG):
            pass_on(t, A)
            pass_on(t, B)
            pass_last(t, A)
            pass_last(t, B)
        own_logits(A, 0, tiles)
        own_logits(B, 0, tiles)
        from_core(TXT, A)
        from_core(TXT, B)
        own_logits(A, tiles, 2 * tiles)
        same_pairs(A)
        image_terms(A)
        own_logits(B, tiles, 2 * tiles)
        same_pairs(B)
        image_terms(B)
        sums_first()
        add_relayed(IMG, A)
        add_relayed(IMG, B)
        from_core(IMG, A)
        other_logits(A)
        from_core(IMG, B)
        other_logits(B)
        text_terms(A)
        sums_next(1)
        text_terms(B)
        sums_next(2)
        add_relayed(TXT, A)
        sums_next(3)
        add_relayed(TXT, B)
        sums_next(4)
        for t in (IMG, TXT):
            for h in (A, B):
                finish(t, h)
                local_out(t, h).start()
        sums_last()
        for t in (IMG, TXT):
            for h in (A, B):
                local_out(t, h).wait()

    @pl.when(jnp.logical_not(native))
    def _():
        z_in(TXT, A).start()
        z_in(TXT, A).wait_send()
        z_in(TXT, B).start()
        z_in(TXT, A).wait_recv()
        send_half(TXT, A)
        z_in(TXT, B).wait_send()
        z_in(IMG, A).start()
        pass_on(TXT, A)
        z_in(TXT, B).wait_recv()
        send_half(TXT, B)
        z_in(IMG, A).wait_send()
        z_in(IMG, B).start()
        pass_last(TXT, A)
        pass_on(TXT, B)
        pass_last(TXT, B)
        from_core(IMG, A)
        from_core(IMG, B)
        other_logits(A)
        z_in(IMG, A).wait_recv()
        send_half(IMG, A)
        other_logits(B)
        from_core(TXT, A)
        from_core(TXT, B)
        pass_on(IMG, A)
        z_in(IMG, B).wait_recv()
        send_half(IMG, B)
        pass_last(IMG, A)
        own_logits(A, 0, tiles)
        pass_on(IMG, B)
        own_logits(A, tiles, 2 * tiles)
        pass_last(IMG, B)
        same_pairs(A)
        image_terms(A)
        own_logits(B, 0, 2 * tiles)
        same_pairs(B)
        text_terms(A)
        sums_first()
        text_terms(B)
        add_relayed(IMG, A)
        image_terms(B)
        sums_next(1)
        add_relayed(TXT, A)
        add_relayed(TXT, B)
        sums_next(2)
        add_relayed(IMG, B)
        sums_next(3)
        finish(IMG, A)
        z_out(IMG, A).start()
        finish(TXT, A)
        z_out(TXT, A).start()
        sums_next(4)
        finish(TXT, B)
        z_out(TXT, B).start()
        finish(IMG, B)
        z_out(IMG, B).start()
        sums_last()
        z_in(IMG, B).wait_send()
        for t in (IMG, TXT):
            for h in (A, B):
                z_out(t, h).wait()

    for t in (TXT, IMG):
        for h in (A, B):
            gather(t, h, 0).wait_send()
            gather(t, h, 1).wait_send()
            relay(t, h).wait_send()
            for index in range(SIDE):
                to_core(t, h, index).wait_send()
            for step in range(3):
                reduce(t, h, step).wait_send()
    for stage in stages:
        for each in stage_copies(*stage):
            each.wait_send()


def per_device(image_embed, text_embed, log_logit_scale, logit_bias):
    rows, width = image_embed.shape
    share = SIDE * rows
    block = share // 2
    pairs = rows * lax.axis_size("blk") * lax.axis_size("dp")
    anywhere, smem = pl.BlockSpec(memory_space=pl.ANY), pl.BlockSpec(memory_space=pltpu.SMEM)
    one = jax.ShapeDtypeStruct((1,), jnp.float32)
    like = jax.ShapeDtypeStruct((rows, width), jnp.bfloat16)
    bf16, f32 = jnp.bfloat16, jnp.float32
    image_gradient, text_gradient, scale_gradient, bias_gradient, loss = pl.pallas_call(
        functools.partial(kernel, pairs),
        out_shape=(like, like, one, one, one),
        in_specs=[smem, smem, anywhere, anywhere],
        out_specs=(anywhere, anywhere, smem, smem, smem),
        scratch_shapes=[
            pltpu.VMEM((2, rows, width), bf16),
            pltpu.VMEM((2, rows, 128), f32),
            pltpu.VMEM((2 * share, width), bf16),
            pltpu.VMEM((2 * share, width), bf16),
            pltpu.VMEM((share, 2 * share), bf16),
            pltpu.VMEM((share, share), bf16),
            pltpu.VMEM((block, TILE), f32),
            pltpu.VMEM((block, TILE), f32),
            pltpu.VMEM((share, width), f32),
            pltpu.VMEM((share, width), f32),
            pltpu.VMEM((2, rows, width), f32),
            pltpu.VMEM((2, rows, width), f32),
            pltpu.VMEM((2, rows // 2, width), f32),
            pltpu.VMEM((2, rows // 2, width), f32),
            pltpu.VMEM((2, rows, width), bf16),
            pltpu.VMEM((3, 8, TILE), f32),
            pltpu.VMEM((4, 24, 128), f32),
            pltpu.VMEM((4, 24, 128), f32),
            pltpu.VMEM((2, 24, 128), f32),
            pltpu.VMEM((4, 24, 128), f32),
            pltpu.VMEM((2, 24, 128), f32),
            pltpu.SemaphoreType.DMA((COPIES,)),
            pltpu.SemaphoreType.DMA((COPIES,)),
            pltpu.SemaphoreType.DMA((6,)),
        ],
        name="contrastive_step",
        compiler_params=pltpu.CompilerParams(
            collective_id=0, has_side_effects=True, vmem_limit_bytes=48 * 2**20
        ),
    )(log_logit_scale, logit_bias, image_embed, text_embed)
    return image_gradient, text_gradient, scale_gradient, bias_gradient, loss


def solution(mesh):
    placed = (P(("blk", "dp"), None), P(("blk", "dp"), None), P(), P())
    return jax.shard_map(
        per_device,
        mesh=mesh,
        in_specs=placed,
        out_specs=(P(("blk", "dp"), None), P(("blk", "dp"), None), P(), P(), P()),
        check_vma=False,
    )
```

```python
import functools

import jax
import jax.numpy as jnp
from jax import lax
from jax.experimental import pallas as pl
from jax.experimental.pallas import tpu as pltpu
from jax.sharding import PartitionSpec as P

EPS = 1e-06
LOG2E = 1.4426950408889634
LN2 = 0.6931471805599453
MESH = pl.DeviceIdType.MESH
SIDE = 4
TILE = 256
TXT, IMG = 0, 1
A, B = 0, 1
OVER_COLS = (((1,), (1,)), ((), ()))
OVER_ROWS = (((0,), (0,)), ((), ()))

Z_IN, GATHER, RELAY, CORE, REDUCE, Z_OUT = 0, 4, 12, 16, 32, 44
ST_X, ST_Y, ST_C, ST_L, ST_P = 48, 51, 54, 55, 58
COPIES = 59


def kernel(
    pairs, log_scale_any, bias_any, img_ref, txt_ref,
    out_img, out_txt, out_totals,
    raw, inverses, texts, images, coef_own, coef_other, cos_even, cos_odd,
    grad_txt, grad_img, recv_txt, recv_img, relay_txt, relay_img,
    final, acc, st_x, st_y, st_c, st_l, st_p, log_scale_ref, bias_ref, send_sem, recv_sem, local_sem, turn,
):
    rows, width = img_ref.shape
    part = rows // 2
    block = SIDE * part
    share = 2 * block
    blk, dp = lax.axis_index("blk"), lax.axis_index("dp")
    zh, x, y = blk // (SIDE * SIDE), (blk // SIDE) % SIDE, blk % SIDE
    zl, core = dp // 2, dp % 2
    native = core == zh

    def device(dx=0, dy=0, dl=0, other_core=False, other_plane=False):
        h = 1 - zh if other_plane else zh
        c = 1 - core if other_core else core
        return {
            "blk": (h * SIDE + (x + dx) % SIDE) * SIDE + (y + dy) % SIDE,
            "dp": ((zl + dl) % SIDE) * 2 + c,
        }

    along_x = [device(dx=d) for d in (1, 2, 3)]
    along_y = [device(dy=d) for d in (1, 2, 3)]
    along_l = [device(dl=d) for d in (1, 2, 3)]
    right = (along_x[0], along_y[0])
    left = (along_x[2], along_y[2])
    sibling = device(other_core=True)
    partner = device(other_core=True, other_plane=True)
    inputs, outputs = (txt_ref, img_ref), (out_txt, out_img)
    units, grads = (texts, images), (grad_txt, grad_img)
    recvs, relays = (recv_txt, recv_img), (relay_txt, relay_img)

    def copy(number, src, dst, where):
        return pltpu.make_async_remote_copy(
            src_ref=src, dst_ref=dst, send_sem=send_sem.at[number], recv_sem=recv_sem.at[number],
            device_id=where, device_id_type=MESH,
        )

    def half(h):
        return pl.ds(h * part, part)

    def slot(h, index, other=0):
        return pl.ds(other * share + h * block + index * part, part)

    def z_in(t, h):
        return copy(Z_IN + 2 * t + h, inputs[t].at[half(h)], raw.at[t, half(h)], partner)

    def gather(t, h, d):
        return copy(
            GATHER + 4 * t + 2 * h + d, units[t].at[slot(h, 0)], units[t].at[slot(h, (3, 1)[d])], (right, left)[d][t]
        )

    def relay(t, h):
        return copy(
            RELAY + 2 * t + h, units[t].at[slot(h, (3, 1)[h])], units[t].at[slot(h, 2)], (right, left)[h][t]
        )

    def to_core(t, h, index):
        return copy(
            CORE + 8 * t + 4 * h + index, units[t].at[slot(h, index)], units[t].at[slot(h, index, 1)], sibling
        )

    def reduce(t, h, step):
        onward = step != 1
        to = (right, left)[h if onward else 1 - h][t]
        if step == 0:
            src, dst = slot(h, 2), relays[t].at[h]
        elif step == 1:
            src, dst = slot(h, (3, 1)[h]), recvs[t].at[1 - h, half(h)]
        else:
            src, dst = slot(h, (1, 3)[h]), recvs[t].at[h, half(h)]
        return copy(REDUCE + 6 * t + 3 * h + step, grads[t].at[src], dst, to)

    def z_out(t, h):
        return copy(Z_OUT + 2 * t + h, final.at[t, half(h)], outputs[t].at[half(h)], partner)

    def local_in(t):
        return pltpu.make_async_copy(inputs[t], raw.at[t], local_sem.at[t])

    def local_out(t, h):
        return pltpu.make_async_copy(final.at[t, half(h)], outputs[t].at[half(h)], local_sem.at[2 + 2 * t + h])

    scalar_copies = [
        pltpu.make_async_copy(src, dst, local_sem.at[6 + i])
        for i, (src, dst) in enumerate(((log_scale_any, log_scale_ref), (bias_any, bias_ref)))
    ]
    for each in scalar_copies:
        each.start()

    @pl.when(native)
    def _():
        local_in(TXT).start()
        local_in(IMG).start()

    barrier = pltpu.get_barrier_semaphore()
    everyone = along_x + along_y + along_l + [sibling, partner]
    for other in everyone:
        pl.semaphore_signal(barrier, inc=1, device_id=other, device_id_type=MESH)
    pl.semaphore_wait(barrier, len(everyone))

    for each in scalar_copies:
        each.wait()
    log_scale = jnp.full((1, TILE), log_scale_ref[0], jnp.float32)
    scale = jnp.exp(log_scale)
    scale2 = scale * LOG2E
    bias2 = jnp.full((1, TILE), bias_ref[0], jnp.float32) * LOG2E
    acc[...] = jnp.zeros_like(acc)

    def normalize(t, h):
        for i in range(part // 32):
            at = pl.ds(h * part + i * 32, 32)
            wide = raw[t, at, :].astype(jnp.float32)
            inverse = lax.rsqrt(jnp.sum(wide * wide, axis=1, keepdims=True) + EPS)
            inverses[t, at, :] = jnp.broadcast_to(inverse, (32, 128))
            units[t][pl.ds(h * block + i * 32, 32), :] = (wide * inverse).astype(jnp.bfloat16)

    def send_half(t, h):
        normalize(t, h)
        gather(t, h, h).start()
        gather(t, h, 1 - h).start()
        to_core(t, h, 0).start()

    def pass_on(t, h):
        gather(t, h, h).wait_recv()
        relay(t, h).start()
        to_core(t, h, (3, 1)[h]).start()
        gather(t, h, 1 - h).wait_recv()
        to_core(t, h, (1, 3)[h]).start()

    def pass_last(t, h):
        relay(t, h).wait_recv()
        to_core(t, h, 2).start()

    def from_core(t, h):
        for index in range(SIDE):
            to_core(t, h, index).wait_recv()

    def dot_tile(out, first, column):
        out[...] = lax.dot_general(
            images[pl.ds(first, block), :],
            texts[pl.ds(pl.multiple_of(column * TILE, TILE), TILE), :],
            OVER_COLS,
            preferred_element_type=jnp.float32,
        )

    def own_terms(cos_ref, h, column):
        at_cols = pl.ds(pl.multiple_of(column * TILE, TILE), TILE)
        losses = temps = biases = jnp.zeros((8, TILE), jnp.float32)
        strip = 16
        for i in range(block // strip):
            cosine = cos_ref[pl.ds(i * strip, strip), :]
            grown = jnp.exp2(scale2 * cosine + bias2)
            more = 1.0 + grown
            coef = grown / more
            coef_own[pl.ds(h * block + i * strip, strip), at_cols] = coef.astype(jnp.bfloat16)
            fold = (strip // 8, 8, TILE)
            losses += jnp.sum(jnp.log(more).reshape(fold), axis=0)
            temps += jnp.sum((coef * cosine).reshape(fold), axis=0)
            biases += jnp.sum(coef.reshape(fold), axis=0)
        acc[0] += losses
        acc[1] += temps
        acc[2] += biases

    def other_terms(cos_ref, h, column):
        at_cols = pl.ds(pl.multiple_of(column * TILE, TILE), TILE)
        strip = 16
        for i in range(block // strip):
            grown = jnp.exp2(scale2 * cos_ref[pl.ds(i * strip, strip), :] + bias2)
            coef_other[pl.ds(h * block + i * strip, strip), at_cols] = (grown / (1.0 + grown)).astype(jnp.bfloat16)

    def sweep(terms, first, h, start, stop):
        dot_tile(cos_even, first, start)
        count = stop - start

        def body(p, _):
            column = start + 2 * p
            dot_tile(cos_odd, first, column + 1)
            terms(cos_even, h, column)
            dot_tile(cos_even, first, jnp.minimum(column + 2, stop - 1))
            terms(cos_odd, h, column + 1)
            return 0

        lax.fori_loop(0, count // 2, body, 0)
        if count % 2:
            terms(cos_even, h, stop - 1)

    def own_logits(h, start, stop):
        sweep(own_terms, h * block, h, start, stop)

    def other_logits(h):
        sweep(other_terms, share + h * block, h, 0, share // TILE)

    def same_pairs(h):
        lanes = 128
        at_rows, at_cols = pl.ds(h * block, part), pl.ds(h * block, lanes)
        cosine = lax.dot_general(
            images[at_rows, :], texts[at_cols, :], OVER_COLS, preferred_element_type=jnp.float32
        )
        shape = (part, lanes)
        same = lax.broadcasted_iota(jnp.int32, shape, 0) == lax.broadcasted_iota(jnp.int32, shape, 1)
        grown = jnp.exp2(scale2[:, :lanes] * cosine + bias2[:, :lanes])
        more = 1.0 + grown
        inverse = 1.0 / more
        coef = grown * inverse
        coef_own[at_rows, at_cols] = jnp.where(same, -inverse, coef).astype(jnp.bfloat16)
        logit = scale[:, :lanes] * cosine + bias_ref[0]
        change = jnp.where(same, -inverse - coef, 0.0)
        fold = (part // 8, 8, lanes)
        acc[0, :, :lanes] += jnp.sum(jnp.where(same, -logit, 0.0).reshape(fold), axis=0)
        acc[1, :, :lanes] += jnp.sum((change * cosine).reshape(fold), axis=0)
        acc[2, :, :lanes] += jnp.sum(change.reshape(fold), axis=0)

    def image_terms(h):
        at_rows = pl.ds(h * block, block)
        grad_img[at_rows, :] = jnp.dot(coef_own[at_rows, :], texts[...], preferred_element_type=jnp.float32)
        reduce(IMG, h, 0).start()
        reduce(IMG, h, 1).start()

    def text_terms(h):
        at_rows = pl.ds(h * block, block)
        grad_txt[at_rows, :] = lax.dot_general(
            coef_own[:, at_rows], images[:share, :], OVER_ROWS, preferred_element_type=jnp.float32
        ) + lax.dot_general(
            coef_other[:, at_rows], images[share:, :], OVER_ROWS, preferred_element_type=jnp.float32
        )

    def text_start(h):
        reduce(TXT, h, 0).start()
        reduce(TXT, h, 1).start()

    def add_relayed(t, h):
        reduce(t, h, 0).wait_recv()
        grads[t][slot(h, (1, 3)[h]), :] += relays[t][h]
        reduce(t, h, 2).start()

    def finish(t, h):
        reduce(t, h, 1).wait_recv()
        reduce(t, h, 2).wait_recv()
        for i in range(part // 16):
            at = pl.ds(h * part + i * 16, 16)
            inverse = inverses[t, at, :1]
            unit = raw[t, at, :].astype(jnp.float32) * inverse
            scaled = scale[:, :1] * (
                grads[t][pl.ds(h * block + i * 16, 16), :] + recvs[t][0, at, :] + recvs[t][1, at, :]
            )
            along = jnp.sum(unit * scaled, axis=1, keepdims=True)
            final[t, at, :] = ((scaled - unit * along) * inverse).astype(jnp.bfloat16)

    stages = (
        (ST_X, st_x, x, along_x),
        (ST_Y, st_y, y, along_y),
        (ST_C, st_c, core, [sibling]),
        (ST_L, st_l, zl, along_l),
        (ST_P, st_p, zh, [partner]),
    )

    def stage_copies(base, buffer, mine, line):
        return [copy(base + i, buffer.at[mine], buffer.at[mine], other) for i, other in enumerate(line)]

    def sums_start(stage, value):
        _, buffer, mine, _ = stages[stage]
        buffer[mine] = value
        for each in stage_copies(*stages[stage]):
            each.start()

    def sums_finish(stage):
        for each in stage_copies(*stages[stage]):
            each.wait_recv()
        buffer, count = stages[stage][1], len(stages[stage][3]) + 1
        return functools.reduce(lambda a, b: a + b, [buffer[i] for i in range(count)])

    def sums_first():
        sums_start(0, (acc[:, :, :128] + acc[:, :, 128:]).reshape(24, 128))

    def sums_next(stage):
        sums_start(stage, sums_finish(stage - 1))

    def sums_last():
        totals = sums_finish(len(stages) - 1)
        for k, factor in enumerate((1.0, scale[:, :1], 1.0)):
            total = jnp.sum(jnp.sum(totals[8 * k : 8 * k + 8], axis=0, keepdims=True), axis=1, keepdims=True)
            out_totals[k : k + 1, :] = jnp.broadcast_to(factor * total / pairs, (1, 128))

    tiles = share // TILE

    def wait_sent(t, steps):
        for h in (A, B):
            for step in steps:
                reduce(t, h, step).wait_send()

    @pl.when(native)
    def _():
        for t in (TXT, IMG):
            local_in(t).wait()
            send_half(t, A)
            send_half(t, B)
        for t in (TXT, IMG):
            pass_on(t, A)
            pass_on(t, B)
            pass_last(t, A)
            pass_last(t, B)
        own_logits(A, 0, tiles)
        own_logits(B, 0, tiles)
        from_core(TXT, A)
        from_core(TXT, B)
        own_logits(A, tiles, 2 * tiles)
        same_pairs(A)
        image_terms(A)
        own_logits(B, tiles, 2 * tiles)
        same_pairs(B)
        image_terms(B)
        sums_first()
        add_relayed(IMG, A)
        add_relayed(IMG, B)
        from_core(IMG, A)
        other_logits(A)
        sums_next(1)
        from_core(IMG, B)
        other_logits(B)
        text_terms(A)
        text_terms(B)
        sums_next(2)
        for h in (A, B):
            finish(IMG, h)
            local_out(IMG, h).start()
        pl.semaphore_wait(turn, 1)
        text_start(A)
        text_start(B)
        sums_next(3)
        add_relayed(TXT, A)
        add_relayed(TXT, B)
        sums_next(4)
        for h in (A, B):
            finish(TXT, h)
            local_out(TXT, h).start()
        sums_last()
        for t in (IMG, TXT):
            for h in (A, B):
                local_out(t, h).wait()
        wait_sent(TXT, (2,))

    @pl.when(jnp.logical_not(native))
    def _():
        z_in(TXT, A).start()
        z_in(TXT, A).wait_send()
        z_in(TXT, B).start()
        z_in(TXT, A).wait_recv()
        send_half(TXT, A)
        z_in(TXT, B).wait_send()
        z_in(IMG, A).start()
        pass_on(TXT, A)
        z_in(TXT, B).wait_recv()
        send_half(TXT, B)
        z_in(IMG, A).wait_send()
        z_in(IMG, B).start()
        pass_last(TXT, A)
        z_in(IMG, A).wait_recv()
        send_half(IMG, A)
        pass_on(TXT, B)
        z_in(IMG, B).wait_recv()
        send_half(IMG, B)
        pass_on(IMG, A)
        pass_last(TXT, B)
        from_core(IMG, A)
        from_core(IMG, B)
        other_logits(A)
        other_logits(B)
        from_core(TXT, A)
        from_core(TXT, B)
        pass_last(IMG, A)
        own_logits(A, 0, tiles)
        pass_on(IMG, B)
        own_logits(A, tiles, 2 * tiles)
        same_pairs(A)
        pass_last(IMG, B)
        image_terms(A)
        own_logits(B, 0, 2 * tiles)
        same_pairs(B)
        text_terms(A)
        text_start(A)
        text_terms(B)
        text_start(B)
        sums_first()
        add_relayed(IMG, A)
        image_terms(B)
        add_relayed(TXT, A)
        add_relayed(TXT, B)
        sums_next(1)
        add_relayed(IMG, B)
        finish(IMG, A)
        z_out(IMG, A).start()
        sums_next(2)
        wait_sent(TXT, (2,))
        pl.semaphore_signal(turn, inc=1, device_id=sibling, device_id_type=MESH)
        finish(TXT, A)
        z_out(TXT, A).start()
        finish(TXT, B)
        z_out(TXT, B).start()
        finish(IMG, B)
        z_out(IMG, B).start()
        sums_next(3)
        sums_next(4)
        sums_last()
        z_in(IMG, B).wait_send()
        for t in (IMG, TXT):
            for h in (A, B):
                z_out(t, h).wait()

    for t in (TXT, IMG):
        for h in (A, B):
            gather(t, h, 0).wait_send()
            gather(t, h, 1).wait_send()
            relay(t, h).wait_send()
            for index in range(SIDE):
                to_core(t, h, index).wait_send()
    wait_sent(TXT, (0, 1))
    wait_sent(IMG, (0, 1, 2))
    for stage in stages:
        for each in stage_copies(*stage):
            each.wait_send()


def per_device(image_embed, text_embed, log_logit_scale, logit_bias):
    rows, width = image_embed.shape
    share = SIDE * rows
    block = share // 2
    pairs = rows * lax.axis_size("blk") * lax.axis_size("dp")
    hbm, vmem = pl.BlockSpec(memory_space=pltpu.HBM), pl.BlockSpec(memory_space=pltpu.VMEM)
    like = jax.ShapeDtypeStruct((rows, width), jnp.bfloat16)
    bf16, f32 = jnp.bfloat16, jnp.float32
    image_gradient, text_gradient, totals = pl.pallas_call(
        functools.partial(kernel, pairs),
        out_shape=(like, like, jax.ShapeDtypeStruct((8, 128), f32)),
        in_specs=[hbm, hbm, hbm, hbm],
        out_specs=(hbm, hbm, vmem),
        scratch_shapes=[
            pltpu.VMEM((2, rows, width), bf16),
            pltpu.VMEM((2, rows, 128), f32),
            pltpu.VMEM((2 * share, width), bf16),
            pltpu.VMEM((2 * share, width), bf16),
            pltpu.VMEM((share, 2 * share), bf16),
            pltpu.VMEM((share, share), bf16),
            pltpu.VMEM((block, TILE), f32),
            pltpu.VMEM((block, TILE), f32),
            pltpu.VMEM((share, width), f32),
            pltpu.VMEM((share, width), f32),
            pltpu.VMEM((2, rows, width), f32),
            pltpu.VMEM((2, rows, width), f32),
            pltpu.VMEM((2, rows // 2, width), f32),
            pltpu.VMEM((2, rows // 2, width), f32),
            pltpu.VMEM((2, rows, width), bf16),
            pltpu.VMEM((3, 8, TILE), f32),
            pltpu.VMEM((4, 24, 128), f32),
            pltpu.VMEM((4, 24, 128), f32),
            pltpu.VMEM((2, 24, 128), f32),
            pltpu.VMEM((4, 24, 128), f32),
            pltpu.VMEM((2, 24, 128), f32),
            pltpu.SMEM((1,), f32),
            pltpu.SMEM((1,), f32),
            pltpu.SemaphoreType.DMA((COPIES,)),
            pltpu.SemaphoreType.DMA((COPIES,)),
            pltpu.SemaphoreType.DMA((8,)),
            pltpu.SemaphoreType.REGULAR,
        ],
        name="contrastive_step",
        compiler_params=pltpu.CompilerParams(
            collective_id=0, has_side_effects=True, vmem_limit_bytes=62 * 2**20
        ),
    )(log_logit_scale, logit_bias, image_embed, text_embed)
    loss, scale_gradient, bias_gradient = totals[0, :1], totals[1, :1], totals[2, :1]
    return image_gradient, text_gradient, scale_gradient, bias_gradient, loss


def solution(mesh):
    placed = (P(("blk", "dp"), None), P(("blk", "dp"), None), P(), P())
    return jax.shard_map(
        per_device,
        mesh=mesh,
        in_specs=placed,
        out_specs=(P(("blk", "dp"), None), P(("blk", "dp"), None), P(), P(), P()),
        check_vma=False,
    )
```

```python
import functools

import jax
import jax.numpy as jnp
from jax import lax
from jax.experimental import pallas as pl
from jax.experimental.pallas import tpu as pltpu
from jax.sharding import PartitionSpec as P

EPS = 1e-06
LOG2E = 1.4426950408889634
LN2 = 0.6931471805599453
MESH = pl.DeviceIdType.MESH
SIDE = 4
TILE = 256
TXT, IMG = 0, 1
A, B = 0, 1
OVER_COLS = (((1,), (1,)), ((), ()))
OVER_ROWS = (((0,), (0,)), ((), ()))

Z_IN, GATHER, ACROSS, CORE, REDUCE, Z_OUT = 0, 4, 12, 16, 32, 44
ST_X, ST_Y, ST_C, ST_L, ST_P = 48, 51, 54, 56, 59
COPIES = 60


def kernel(
    pairs, log_scale_any, bias_any, img_ref, txt_ref,
    out_img, out_txt, out_totals,
    raw, inverses, texts, images, coef_own, coef_other, cos_even, cos_odd,
    grad_txt, grad_img, recv_txt, recv_img, relay_txt, relay_img,
    final, acc, st_x, st_y, st_c, st_l, st_p, log_scale_ref, bias_ref, send_sem, recv_sem, local_sem, turn,
):
    rows, width = img_ref.shape
    part = rows // 2
    block = SIDE * part
    share = 2 * block
    blk, dp = lax.axis_index("blk"), lax.axis_index("dp")
    zh, x, y = blk // (SIDE * SIDE), (blk // SIDE) % SIDE, blk % SIDE
    zl, core = dp // 2, dp % 2
    native = core == zh

    def device(dx=0, dy=0, dl=0, other_core=False, other_plane=False):
        h = 1 - zh if other_plane else zh
        c = 1 - core if other_core else core
        return {
            "blk": (h * SIDE + (x + dx) % SIDE) * SIDE + (y + dy) % SIDE,
            "dp": ((zl + dl) % SIDE) * 2 + c,
        }

    along_x = [device(dx=d) for d in (1, 2, 3)]
    along_y = [device(dy=d) for d in (1, 2, 3)]
    along_l = [device(dl=d) for d in (1, 2, 3)]
    right = (along_x[0], along_y[0])
    left = (along_x[2], along_y[2])
    sibling = device(other_core=True)
    partner = device(other_core=True, other_plane=True)
    inputs, outputs = (txt_ref, img_ref), (out_txt, out_img)
    units, grads = (texts, images), (grad_txt, grad_img)
    recvs, relays = (recv_txt, recv_img), (relay_txt, relay_img)

    def copy(number, src, dst, where):
        return pltpu.make_async_remote_copy(
            src_ref=src, dst_ref=dst, send_sem=send_sem.at[number], recv_sem=recv_sem.at[number],
            device_id=where, device_id_type=MESH,
        )

    def half(h):
        return pl.ds(h * part, part)

    def slot(h, index, other=0):
        return pl.ds(other * share + h * block + index * part, part)

    def z_in(t, h):
        return copy(Z_IN + 2 * t + h, inputs[t].at[half(h)], raw.at[t, half(h)], partner)

    def gather(t, h, d):
        return copy(
            GATHER + 4 * t + 2 * h + d, units[t].at[slot(h, 0)], units[t].at[slot(h, (3, 1)[d])], (right, left)[d][t]
        )

    def across(t, h):
        return copy(
            ACROSS + 2 * t + h, units[t].at[slot(h, 0)], units[t].at[slot(h, 2)], (along_x, along_y)[t][1]
        )

    def to_core(t, h, index):
        return copy(
            CORE + 8 * t + 4 * h + index, units[t].at[slot(h, index)], units[t].at[slot(h, index, 1)], sibling
        )

    def reduce(t, h, step):
        onward = step != 1
        to = (right, left)[h if onward else 1 - h][t]
        if step == 0:
            src, dst = slot(h, 2), relays[t].at[h]
        elif step == 1:
            src, dst = slot(h, (3, 1)[h]), recvs[t].at[1 - h, half(h)]
        else:
            src, dst = slot(h, (1, 3)[h]), recvs[t].at[h, half(h)]
        return copy(REDUCE + 6 * t + 3 * h + step, grads[t].at[src], dst, to)

    def z_out(t, h):
        return copy(Z_OUT + 2 * t + h, final.at[t, half(h)], outputs[t].at[half(h)], partner)

    def local_in(t):
        return pltpu.make_async_copy(inputs[t], raw.at[t], local_sem.at[t])

    def local_out(t, h):
        return pltpu.make_async_copy(final.at[t, half(h)], outputs[t].at[half(h)], local_sem.at[2 + 2 * t + h])

    scalar_copies = [
        pltpu.make_async_copy(src, dst, local_sem.at[6 + i])
        for i, (src, dst) in enumerate(((log_scale_any, log_scale_ref), (bias_any, bias_ref)))
    ]
    for each in scalar_copies:
        each.start()

    @pl.when(native)
    def _():
        local_in(TXT).start()
        local_in(IMG).start()

    barrier = pltpu.get_barrier_semaphore()
    everyone = along_x + along_y + along_l + [sibling, partner]
    for other in everyone:
        pl.semaphore_signal(barrier, inc=1, device_id=other, device_id_type=MESH)
    pl.semaphore_wait(barrier, len(everyone))

    for each in scalar_copies:
        each.wait()
    log_scale = jnp.full((1, TILE), log_scale_ref[0], jnp.float32)
    scale = jnp.exp(log_scale)
    scale2 = scale * LOG2E
    bias2 = jnp.full((1, TILE), bias_ref[0], jnp.float32) * LOG2E
    acc[...] = jnp.zeros_like(acc)

    def normalize(t, h):
        for i in range(part // 32):
            at = pl.ds(h * part + i * 32, 32)
            wide = raw[t, at, :].astype(jnp.float32)
            inverse = lax.rsqrt(jnp.sum(wide * wide, axis=1, keepdims=True) + EPS)
            inverses[t, at, :] = jnp.broadcast_to(inverse, (32, 128))
            units[t][pl.ds(h * block + i * 32, 32), :] = (wide * inverse).astype(jnp.bfloat16)

    def send_half(t, h):
        normalize(t, h)
        across(t, h).start()
        gather(t, h, 0).start()
        gather(t, h, 1).start()
        to_core(t, h, 0).start()

    def pass_on(t, h):
        for index, landed in ((3, gather(t, h, 0)), (1, gather(t, h, 1)), (2, across(t, h))):
            landed.wait_recv()
            to_core(t, h, index).start()

    def from_core(t, h):
        for index in range(SIDE):
            to_core(t, h, index).wait_recv()

    def dot_tile(out, first, column):
        out[...] = lax.dot_general(
            images[pl.ds(first, block), :],
            texts[pl.ds(pl.multiple_of(column * TILE, TILE), TILE), :],
            OVER_COLS,
            preferred_element_type=jnp.float32,
        )

    def own_terms(cos_ref, h, column):
        at_cols = pl.ds(pl.multiple_of(column * TILE, TILE), TILE)
        losses = temps = biases = jnp.zeros((8, TILE), jnp.float32)
        strip = 16
        for i in range(block // strip):
            cosine = cos_ref[pl.ds(i * strip, strip), :]
            grown = jnp.exp2(scale2 * cosine + bias2)
            more = 1.0 + grown
            coef = grown / more
            coef_own[pl.ds(h * block + i * strip, strip), at_cols] = coef.astype(jnp.bfloat16)
            fold = (strip // 8, 8, TILE)
            losses += jnp.sum(jnp.log(more).reshape(fold), axis=0)
            temps += jnp.sum((coef * cosine).reshape(fold), axis=0)
            biases += jnp.sum(coef.reshape(fold), axis=0)
        acc[0] += losses
        acc[1] += temps
        acc[2] += biases

    def other_terms(cos_ref, h, column):
        at_cols = pl.ds(pl.multiple_of(column * TILE, TILE), TILE)
        strip = 16
        for i in range(block // strip):
            grown = jnp.exp2(scale2 * cos_ref[pl.ds(i * strip, strip), :] + bias2)
            coef_other[pl.ds(h * block + i * strip, strip), at_cols] = (grown / (1.0 + grown)).astype(jnp.bfloat16)

    def sweep(terms, first, h, start, stop):
        dot_tile(cos_even, first, start)
        count = stop - start

        def body(p, _):
            column = start + 2 * p
            dot_tile(cos_odd, first, column + 1)
            terms(cos_even, h, column)
            dot_tile(cos_even, first, jnp.minimum(column + 2, stop - 1))
            terms(cos_odd, h, column + 1)
            return 0

        lax.fori_loop(0, count // 2, body, 0)
        if count % 2:
            terms(cos_even, h, stop - 1)

    def own_logits(h, start, stop):
        sweep(own_terms, h * block, h, start, stop)

    def other_logits(h):
        sweep(other_terms, share + h * block, h, 0, share // TILE)

    def same_pairs(h):
        lanes = 128
        at_rows, at_cols = pl.ds(h * block, part), pl.ds(h * block, lanes)
        cosine = lax.dot_general(
            images[at_rows, :], texts[at_cols, :], OVER_COLS, preferred_element_type=jnp.float32
        )
        shape = (part, lanes)
        same = lax.broadcasted_iota(jnp.int32, shape, 0) == lax.broadcasted_iota(jnp.int32, shape, 1)
        grown = jnp.exp2(scale2[:, :lanes] * cosine + bias2[:, :lanes])
        more = 1.0 + grown
        inverse = 1.0 / more
        coef = grown * inverse
        coef_own[at_rows, at_cols] = jnp.where(same, -inverse, coef).astype(jnp.bfloat16)
        logit = scale[:, :lanes] * cosine + bias_ref[0]
        change = jnp.where(same, -inverse - coef, 0.0)
        fold = (part // 8, 8, lanes)
        acc[0, :, :lanes] += jnp.sum(jnp.where(same, -logit, 0.0).reshape(fold), axis=0)
        acc[1, :, :lanes] += jnp.sum((change * cosine).reshape(fold), axis=0)
        acc[2, :, :lanes] += jnp.sum(change.reshape(fold), axis=0)

    def image_terms(h):
        at_rows = pl.ds(h * block, block)
        grad_img[at_rows, :] = jnp.dot(coef_own[at_rows, :], texts[...], preferred_element_type=jnp.float32)

    def turned_dot(coefs, units_rows):
        return lax.dot_general(coefs, units_rows, OVER_ROWS, preferred_element_type=jnp.float32)

    def text_early(h):
        at_rows = pl.ds(h * block, block)
        grad_txt[at_rows, :] = turned_dot(coef_own[:block, at_rows], images[:block, :]) + turned_dot(
            coef_other[:, at_rows], images[share:, :]
        )

    def text_late(h):
        at_rows = pl.ds(h * block, block)
        grad_txt[at_rows, :] += turned_dot(coef_own[block:, at_rows], images[block:share, :])

    def text_terms(h):
        at_rows = pl.ds(h * block, block)
        grad_txt[at_rows, :] = turned_dot(coef_own[:, at_rows], images[:share, :]) + turned_dot(
            coef_other[:, at_rows], images[share:, :]
        )

    def add_relayed(t, h):
        reduce(t, h, 0).wait_recv()
        grads[t][slot(h, (1, 3)[h]), :] += relays[t][h]
        reduce(t, h, 2).start()

    def finish(t, h):
        reduce(t, h, 1).wait_recv()
        reduce(t, h, 2).wait_recv()
        for i in range(part // 16):
            at = pl.ds(h * part + i * 16, 16)
            inverse = inverses[t, at, :1]
            unit = raw[t, at, :].astype(jnp.float32) * inverse
            scaled = scale[:, :1] * (
                grads[t][pl.ds(h * block + i * 16, 16), :] + recvs[t][0, at, :] + recvs[t][1, at, :]
            )
            along = jnp.sum(unit * scaled, axis=1, keepdims=True)
            final[t, at, :] = ((scaled - unit * along) * inverse).astype(jnp.bfloat16)

    stages = ((ST_X, st_x, x, along_x), (ST_Y, st_y, y, along_y), (ST_L, st_l, zl, along_l), (ST_P, st_p, zh, [partner]))
    to_native = copy(ST_C, st_c.at[0], st_c.at[1], sibling)
    to_foreign = copy(ST_C + 1, st_c.at[0], st_c.at[1], sibling)

    def own_sums():
        return (acc[:, :, :128] + acc[:, :, 128:]).reshape(24, 128)

    def stage_copies(base, buffer, mine, line):
        return [copy(base + i, buffer.at[mine], buffer.at[mine], other) for i, other in enumerate(line)]

    def sums_start(stage, value):
        _, buffer, mine, _ = stages[stage]
        buffer[mine] = value
        for each in stage_copies(*stages[stage]):
            each.start()

    def sums_finish(stage):
        for each in stage_copies(*stages[stage]):
            each.wait_recv()
        buffer, count = stages[stage][1], len(stages[stage][3]) + 1
        return functools.reduce(lambda a, b: a + b, [buffer[i] for i in range(count)])

    def write_totals(totals):
        for k, factor in enumerate((1.0, scale[:, :1], 1.0)):
            total = jnp.sum(jnp.sum(totals[8 * k : 8 * k + 8], axis=0, keepdims=True), axis=1, keepdims=True)
            out_totals[k : k + 1, :] = jnp.broadcast_to(factor * total / pairs, (1, 128))

    tiles = share // TILE

    def wait_sent(t, steps):
        for h in (A, B):
            for step in steps:
                reduce(t, h, step).wait_send()

    def start_both(t, step):
        reduce(t, A, step).start()
        reduce(t, B, step).start()

    def wait_sent(t, steps):
        for step in steps:
            reduce(t, A, step).wait_send()
            reduce(t, B, step).wait_send()

    @pl.when(native)
    def _():
        for t in (TXT, IMG):
            local_in(t).wait()
            send_half(t, A)
            send_half(t, B)
        for t in (TXT, IMG):
            pass_on(t, A)
            pass_on(t, B)
        own_logits(A, 0, tiles)
        own_logits(B, 0, tiles)
        from_core(TXT, A)
        from_core(TXT, B)
        own_logits(A, tiles, 2 * tiles)
        same_pairs(A)
        own_logits(B, tiles, 2 * tiles)
        same_pairs(B)
        image_terms(A)
        image_terms(B)
        from_core(IMG, A)
        other_logits(A)
        to_native.wait_recv()
        sums_start(0, own_sums() + st_c[1])
        from_core(IMG, B)
        other_logits(B)
        sums_start(1, sums_finish(0))
        text_terms(A)
        text_terms(B)
        sums_start(2, sums_finish(1))
        sums_start(3, sums_finish(2))
        totals = sums_finish(3)
        st_c[0] = totals
        to_foreign.start()
        write_totals(totals)
        for t in (TXT, IMG):
            pl.semaphore_wait(turn.at[t], 1)
            start_both(t, 0)
        for t in (TXT, IMG):
            wait_sent(t, (0,))
            start_both(t, 1)
        for t in (TXT, IMG):
            add_relayed(t, A)
            add_relayed(t, B)
        for t in (TXT, IMG):
            for h in (A, B):
                finish(t, h)
                local_out(t, h).start()
        to_foreign.wait_send()
        for stage in stages:
            for each in stage_copies(*stage):
                each.wait_send()
        for t in (TXT, IMG):
            wait_sent(t, (1, 2))
            for h in (A, B):
                local_out(t, h).wait()

    @pl.when(jnp.logical_not(native))
    def _():
        z_in(TXT, A).start()
        z_in(TXT, A).wait_send()
        z_in(TXT, B).start()
        z_in(TXT, A).wait_recv()
        send_half(TXT, A)
        z_in(TXT, B).wait_send()
        z_in(IMG, A).start()
        z_in(TXT, B).wait_recv()
        send_half(TXT, B)
        z_in(IMG, A).wait_send()
        z_in(IMG, B).start()
        pass_on(TXT, A)
        z_in(IMG, A).wait_recv()
        send_half(IMG, A)
        pass_on(TXT, B)
        from_core(IMG, A)
        from_core(IMG, B)
        other_logits(A)
        z_in(IMG, B).wait_recv()
        send_half(IMG, B)
        other_logits(B)
        from_core(TXT, A)
        from_core(TXT, B)
        pass_on(IMG, A)
        own_logits(A, 0, 2 * tiles)
        same_pairs(A)
        image_terms(A)
        reduce(IMG, A, 0).start()
        reduce(IMG, A, 1).start()
        text_early(A)
        text_early(B)
        pass_on(IMG, B)
        own_logits(B, 0, 2 * tiles)
        same_pairs(B)
        st_c[0] = own_sums()
        to_native.start()
        text_late(A)
        reduce(TXT, A, 0).start()
        text_late(B)
        reduce(TXT, B, 0).start()
        add_relayed(IMG, A)
        image_terms(B)
        reduce(IMG, B, 0).start()
        reduce(IMG, B, 1).start()
        wait_sent(TXT, (0,))
        start_both(TXT, 1)
        add_relayed(TXT, A)
        add_relayed(TXT, B)
        finish(IMG, A)
        z_out(IMG, A).start()
        add_relayed(IMG, B)
        wait_sent(TXT, (2,))
        pl.semaphore_signal(turn.at[TXT], inc=1, device_id=sibling, device_id_type=MESH)
        finish(TXT, A)
        z_out(TXT, A).start()
        finish(TXT, B)
        z_out(TXT, B).start()
        wait_sent(IMG, (2,))
        pl.semaphore_signal(turn.at[IMG], inc=1, device_id=sibling, device_id_type=MESH)
        finish(IMG, B)
        z_out(IMG, B).start()
        to_foreign.wait_recv()
        write_totals(st_c[1])
        to_native.wait_send()
        z_in(IMG, B).wait_send()
        wait_sent(TXT, (1,))
        wait_sent(IMG, (0, 1))
        for t in (IMG, TXT):
            for h in (A, B):
                z_out(t, h).wait()

    for t in (TXT, IMG):
        for h in (A, B):
            gather(t, h, 0).wait_send()
            gather(t, h, 1).wait_send()
            across(t, h).wait_send()
            for index in range(SIDE):
                to_core(t, h, index).wait_send()


def per_device(image_embed, text_embed, log_logit_scale, logit_bias):
    rows, width = image_embed.shape
    share = SIDE * rows
    block = share // 2
    pairs = rows * lax.axis_size("blk") * lax.axis_size("dp")
    hbm, vmem = pl.BlockSpec(memory_space=pltpu.HBM), pl.BlockSpec(memory_space=pltpu.VMEM)
    like = jax.ShapeDtypeStruct((rows, width), jnp.bfloat16)
    bf16, f32 = jnp.bfloat16, jnp.float32
    image_gradient, text_gradient, totals = pl.pallas_call(
        functools.partial(kernel, pairs),
        out_shape=(like, like, jax.ShapeDtypeStruct((8, 128), f32)),
        in_specs=[hbm, hbm, hbm, hbm],
        out_specs=(hbm, hbm, vmem),
        scratch_shapes=[
            pltpu.VMEM((2, rows, width), bf16),
            pltpu.VMEM((2, rows, 128), f32),
            pltpu.VMEM((2 * share, width), bf16),
            pltpu.VMEM((2 * share, width), bf16),
            pltpu.VMEM((share, 2 * share), bf16),
            pltpu.VMEM((share, share), bf16),
            pltpu.VMEM((block, TILE), f32),
            pltpu.VMEM((block, TILE), f32),
            pltpu.VMEM((share, width), f32),
            pltpu.VMEM((share, width), f32),
            pltpu.VMEM((2, rows, width), f32),
            pltpu.VMEM((2, rows, width), f32),
            pltpu.VMEM((2, rows // 2, width), f32),
            pltpu.VMEM((2, rows // 2, width), f32),
            pltpu.VMEM((2, rows, width), bf16),
            pltpu.VMEM((3, 8, TILE), f32),
            pltpu.VMEM((4, 24, 128), f32),
            pltpu.VMEM((4, 24, 128), f32),
            pltpu.VMEM((2, 24, 128), f32),
            pltpu.VMEM((4, 24, 128), f32),
            pltpu.VMEM((2, 24, 128), f32),
            pltpu.SMEM((1,), f32),
            pltpu.SMEM((1,), f32),
            pltpu.SemaphoreType.DMA((COPIES,)),
            pltpu.SemaphoreType.DMA((COPIES,)),
            pltpu.SemaphoreType.DMA((8,)),
            pltpu.SemaphoreType.REGULAR((2,)),
        ],
        name="contrastive_step",
        compiler_params=pltpu.CompilerParams(
            collective_id=0, has_side_effects=True, vmem_limit_bytes=62 * 2**20
        ),
    )(log_logit_scale, logit_bias, image_embed, text_embed)
    loss, scale_gradient, bias_gradient = totals[0, :1], totals[1, :1], totals[2, :1]
    return image_gradient, text_gradient, scale_gradient, bias_gradient, loss


def solution(mesh):
    placed = (P(("blk", "dp"), None), P(("blk", "dp"), None), P(), P())
    return jax.shard_map(
        per_device,
        mesh=mesh,
        in_specs=placed,
        out_specs=(P(("blk", "dp"), None), P(("blk", "dp"), None), P(), P(), P()),
        check_vma=False,
    )
```

```python
import functools

import jax
import jax.numpy as jnp
from jax import lax
from jax.experimental import pallas as pl
from jax.experimental.pallas import tpu as pltpu
from jax.sharding import PartitionSpec as P

EPS = 1e-06
LOG2E = 1.4426950408889634
LN2 = 0.6931471805599453
MESH = pl.DeviceIdType.MESH
SIDE = 4
TILE = 256
TXT, IMG = 0, 1
A, B = 0, 1
OVER_COLS = (((1,), (1,)), ((), ()))
OVER_ROWS = (((0,), (0,)), ((), ()))

Z_IN, GATHER, ACROSS, CORE, REDUCE, Z_OUT = 0, 4, 12, 16, 32, 44
ST_X, ST_Y, ST_C, ST_L, ST_P = 48, 51, 54, 56, 59
COPIES = 60


def kernel(
    pairs, log_scale_any, bias_any, img_ref, txt_ref,
    out_grads, out_totals,
    raw, inverses, texts, images, coef_own, coef_other, cos_even, cos_odd,
    grad_txt, grad_img, recv_txt, recv_img, relay_txt, relay_img,
    final, acc, st_x, st_y, st_c, st_l, st_p, log_scale_ref, bias_ref, send_sem, recv_sem, local_sem, turn,
):
    rows, width = img_ref.shape
    part = rows // 2
    block = SIDE * part
    share = 2 * block
    blk, dp = lax.axis_index("blk"), lax.axis_index("dp")
    zh, x, y = blk // (SIDE * SIDE), (blk // SIDE) % SIDE, blk % SIDE
    zl, core = dp // 2, dp % 2
    native = core == zh

    def device(dx=0, dy=0, dl=0, other_core=False, other_plane=False):
        h = 1 - zh if other_plane else zh
        c = 1 - core if other_core else core
        return {
            "blk": (h * SIDE + (x + dx) % SIDE) * SIDE + (y + dy) % SIDE,
            "dp": ((zl + dl) % SIDE) * 2 + c,
        }

    along_x = [device(dx=d) for d in (1, 2, 3)]
    along_y = [device(dy=d) for d in (1, 2, 3)]
    along_l = [device(dl=d) for d in (1, 2, 3)]
    right = (along_x[0], along_y[0])
    left = (along_x[2], along_y[2])
    sibling = device(other_core=True)
    partner = device(other_core=True, other_plane=True)
    inputs, outputs = (txt_ref, img_ref), (out_grads.at[TXT], out_grads.at[IMG])
    units, grads = (texts, images), (grad_txt, grad_img)
    recvs, relays = (recv_txt, recv_img), (relay_txt, relay_img)

    def copy(number, src, dst, where):
        return pltpu.make_async_remote_copy(
            src_ref=src, dst_ref=dst, send_sem=send_sem.at[number], recv_sem=recv_sem.at[number],
            device_id=where, device_id_type=MESH,
        )

    def half(h):
        return pl.ds(h * part, part)

    def slot(h, index, other=0):
        return pl.ds(other * share + h * block + index * part, part)

    def z_in(t, h):
        return copy(Z_IN + 2 * t + h, inputs[t].at[half(h)], raw.at[t, half(h)], partner)

    def gather(t, h, d):
        return copy(
            GATHER + 4 * t + 2 * h + d, units[t].at[slot(h, 0)], units[t].at[slot(h, (3, 1)[d])], (right, left)[d][t]
        )

    def across(t, h):
        return copy(
            ACROSS + 2 * t + h, units[t].at[slot(h, 0)], units[t].at[slot(h, 2)], (along_x, along_y)[t][1]
        )

    def to_core(t, h, index):
        return copy(
            CORE + 8 * t + 4 * h + index, units[t].at[slot(h, index)], units[t].at[slot(h, index, 1)], sibling
        )

    def reduce(t, h, step):
        onward = step != 1
        to = (right, left)[h if onward else 1 - h][t]
        if step == 0:
            src, dst = slot(h, 2), relays[t].at[h]
        elif step == 1:
            src, dst = slot(h, (3, 1)[h]), recvs[t].at[1 - h, half(h)]
        else:
            src, dst = slot(h, (1, 3)[h]), recvs[t].at[h, half(h)]
        return copy(REDUCE + 6 * t + 3 * h + step, grads[t].at[src], dst, to)

    def z_out(t, h):
        return copy(Z_OUT + 2 * t + h, final.at[t, half(h)], outputs[t].at[half(h)], partner)

    def local_in(t):
        return pltpu.make_async_copy(inputs[t], raw.at[t], local_sem.at[t])

    def local_out(t, h):
        return pltpu.make_async_copy(final.at[t, half(h)], outputs[t].at[half(h)], local_sem.at[2 + 2 * t + h])

    scalar_copies = [
        pltpu.make_async_copy(src, dst, local_sem.at[6 + i])
        for i, (src, dst) in enumerate(((log_scale_any, log_scale_ref), (bias_any, bias_ref)))
    ]
    for each in scalar_copies:
        each.start()

    @pl.when(native)
    def _():
        local_in(TXT).start()
        local_in(IMG).start()

    barrier = pltpu.get_barrier_semaphore()
    everyone = along_x + along_y + along_l + [sibling, partner]
    for other in everyone:
        pl.semaphore_signal(barrier, inc=1, device_id=other, device_id_type=MESH)
    pl.semaphore_wait(barrier, len(everyone))

    for each in scalar_copies:
        each.wait()
    log_scale = jnp.full((1, TILE), log_scale_ref[0], jnp.float32)
    scale = jnp.exp(log_scale)
    scale2 = scale * LOG2E
    bias2 = jnp.full((1, TILE), bias_ref[0], jnp.float32) * LOG2E
    acc[...] = jnp.zeros_like(acc)

    def normalize(t, h):
        for i in range(part // 32):
            at = pl.ds(h * part + i * 32, 32)
            wide = raw[t, at, :].astype(jnp.float32)
            inverse = lax.rsqrt(jnp.sum(wide * wide, axis=1, keepdims=True) + EPS)
            inverses[t, at, :] = jnp.broadcast_to(inverse, (32, 128))
            units[t][pl.ds(h * block + i * 32, 32), :] = (wide * inverse).astype(jnp.bfloat16)

    def send_half(t, h):
        normalize(t, h)
        across(t, h).start()
        gather(t, h, 0).start()
        gather(t, h, 1).start()
        to_core(t, h, 0).start()

    def pass_on(t, h):
        for index, landed in ((3, gather(t, h, 0)), (1, gather(t, h, 1)), (2, across(t, h))):
            landed.wait_recv()
            to_core(t, h, index).start()

    def from_core(t, h):
        for index in range(SIDE):
            to_core(t, h, index).wait_recv()

    def dot_tile(out, first, column):
        out[...] = lax.dot_general(
            images[pl.ds(first, block), :],
            texts[pl.ds(pl.multiple_of(column * TILE, TILE), TILE), :],
            OVER_COLS,
            preferred_element_type=jnp.float32,
        )

    def own_terms(cos_ref, h, column):
        at_cols = pl.ds(pl.multiple_of(column * TILE, TILE), TILE)
        losses = temps = biases = jnp.zeros((8, TILE), jnp.float32)
        strip = 16
        for i in range(block // strip):
            cosine = cos_ref[pl.ds(i * strip, strip), :]
            grown = jnp.exp2(scale2 * cosine + bias2)
            more = 1.0 + grown
            coef = grown / more
            coef_own[pl.ds(h * block + i * strip, strip), at_cols] = coef.astype(jnp.bfloat16)
            fold = (strip // 8, 8, TILE)
            losses += jnp.sum(jnp.log(more).reshape(fold), axis=0)
            temps += jnp.sum((coef * cosine).reshape(fold), axis=0)
            biases += jnp.sum(coef.reshape(fold), axis=0)
        acc[0] += losses
        acc[1] += temps
        acc[2] += biases

    def other_terms(cos_ref, h, column):
        at_cols = pl.ds(pl.multiple_of(column * TILE, TILE), TILE)
        strip = 16
        for i in range(block // strip):
            grown = jnp.exp2(scale2 * cos_ref[pl.ds(i * strip, strip), :] + bias2)
            coef_other[pl.ds(h * block + i * strip, strip), at_cols] = (grown / (1.0 + grown)).astype(jnp.bfloat16)

    def sweep(terms, first, h, start, stop):
        dot_tile(cos_even, first, start)
        count = stop - start

        def body(p, _):
            column = start + 2 * p
            dot_tile(cos_odd, first, column + 1)
            terms(cos_even, h, column)
            dot_tile(cos_even, first, jnp.minimum(column + 2, stop - 1))
            terms(cos_odd, h, column + 1)
            return 0

        lax.fori_loop(0, count // 2, body, 0)
        if count % 2:
            terms(cos_even, h, stop - 1)

    def own_logits(h, start, stop):
        sweep(own_terms, h * block, h, start, stop)

    def other_logits(h):
        sweep(other_terms, share + h * block, h, 0, share // TILE)

    def same_pairs(h):
        lanes = 128
        at_rows, at_cols = pl.ds(h * block, part), pl.ds(h * block, lanes)
        cosine = lax.dot_general(
            images[at_rows, :], texts[at_cols, :], OVER_COLS, preferred_element_type=jnp.float32
        )
        shape = (part, lanes)
        same = lax.broadcasted_iota(jnp.int32, shape, 0) == lax.broadcasted_iota(jnp.int32, shape, 1)
        grown = jnp.exp2(scale2[:, :lanes] * cosine + bias2[:, :lanes])
        more = 1.0 + grown
        inverse = 1.0 / more
        coef = grown * inverse
        coef_own[at_rows, at_cols] = jnp.where(same, -inverse, coef).astype(jnp.bfloat16)
        logit = scale[:, :lanes] * cosine + bias_ref[0]
        change = jnp.where(same, -inverse - coef, 0.0)
        fold = (part // 8, 8, lanes)
        acc[0, :, :lanes] += jnp.sum(jnp.where(same, -logit, 0.0).reshape(fold), axis=0)
        acc[1, :, :lanes] += jnp.sum((change * cosine).reshape(fold), axis=0)
        acc[2, :, :lanes] += jnp.sum(change.reshape(fold), axis=0)

    def image_terms(h):
        at_rows = pl.ds(h * block, block)
        grad_img[at_rows, :] = jnp.dot(coef_own[at_rows, :], texts[...], preferred_element_type=jnp.float32)

    def turned_dot(coefs, units_rows):
        return lax.dot_general(coefs, units_rows, OVER_ROWS, preferred_element_type=jnp.float32)

    def text_early(h):
        at_rows = pl.ds(h * block, block)
        grad_txt[at_rows, :] = turned_dot(coef_own[:block, at_rows], images[:block, :]) + turned_dot(
            coef_other[:, at_rows], images[share:, :]
        )

    def text_late(h):
        at_rows = pl.ds(h * block, block)
        grad_txt[at_rows, :] += turned_dot(coef_own[block:, at_rows], images[block:share, :])

    def text_terms(h):
        at_rows = pl.ds(h * block, block)
        grad_txt[at_rows, :] = turned_dot(coef_own[:, at_rows], images[:share, :]) + turned_dot(
            coef_other[:, at_rows], images[share:, :]
        )

    def add_relayed(t, h):
        reduce(t, h, 0).wait_recv()
        grads[t][slot(h, (1, 3)[h]), :] += relays[t][h]
        reduce(t, h, 2).start()

    def finish(t, h):
        reduce(t, h, 1).wait_recv()
        reduce(t, h, 2).wait_recv()
        for i in range(part // 16):
            at = pl.ds(h * part + i * 16, 16)
            inverse = inverses[t, at, :1]
            unit = raw[t, at, :].astype(jnp.float32) * inverse
            scaled = scale[:, :1] * (
                grads[t][pl.ds(h * block + i * 16, 16), :] + recvs[t][0, at, :] + recvs[t][1, at, :]
            )
            along = jnp.sum(unit * scaled, axis=1, keepdims=True)
            final[t, at, :] = ((scaled - unit * along) * inverse).astype(jnp.bfloat16)

    stages = ((ST_X, st_x, x, along_x), (ST_Y, st_y, y, along_y), (ST_L, st_l, zl, along_l), (ST_P, st_p, zh, [partner]))
    to_native = copy(ST_C, st_c.at[0], st_c.at[1], sibling)
    to_foreign = copy(ST_C + 1, st_c.at[0], st_c.at[1], sibling)

    def own_sums():
        return (acc[:, :, :128] + acc[:, :, 128:]).reshape(24, 128)

    def stage_copies(base, buffer, mine, line):
        return [copy(base + i, buffer.at[mine], buffer.at[mine], other) for i, other in enumerate(line)]

    def sums_start(stage, value):
        _, buffer, mine, _ = stages[stage]
        buffer[mine] = value
        for each in stage_copies(*stages[stage]):
            each.start()

    def sums_finish(stage):
        for each in stage_copies(*stages[stage]):
            each.wait_recv()
        buffer, count = stages[stage][1], len(stages[stage][3]) + 1
        return functools.reduce(lambda a, b: a + b, [buffer[i] for i in range(count)])

    def write_totals(totals):
        for k, factor in enumerate((1.0, scale[:, :1], 1.0)):
            total = jnp.sum(jnp.sum(totals[8 * k : 8 * k + 8], axis=0, keepdims=True), axis=1, keepdims=True)
            out_totals[k : k + 1, :] = jnp.broadcast_to(factor * total / pairs, (1, 128))

    tiles = share // TILE

    def wait_sent(t, steps):
        for h in (A, B):
            for step in steps:
                reduce(t, h, step).wait_send()

    def start_both(t, step):
        reduce(t, A, step).start()
        reduce(t, B, step).start()

    def wait_sent(t, steps):
        for step in steps:
            reduce(t, A, step).wait_send()
            reduce(t, B, step).wait_send()

    @pl.when(native)
    def _():
        for t in (TXT, IMG):
            local_in(t).wait()
            send_half(t, A)
            send_half(t, B)
        for t in (TXT, IMG):
            pass_on(t, A)
            pass_on(t, B)
        own_logits(A, 0, tiles)
        own_logits(B, 0, tiles)
        from_core(TXT, A)
        from_core(TXT, B)
        own_logits(A, tiles, 2 * tiles)
        same_pairs(A)
        own_logits(B, tiles, 2 * tiles)
        same_pairs(B)
        image_terms(A)
        image_terms(B)
        from_core(IMG, A)
        other_logits(A)
        to_native.wait_recv()
        sums_start(0, own_sums() + st_c[1])
        from_core(IMG, B)
        other_logits(B)
        sums_start(1, sums_finish(0))
        text_terms(A)
        text_terms(B)
        sums_start(2, sums_finish(1))
        sums_start(3, sums_finish(2))
        totals = sums_finish(3)
        st_c[0] = totals
        to_foreign.start()
        write_totals(totals)
        for t in (TXT, IMG):
            pl.semaphore_wait(turn.at[t], 1)
            start_both(t, 0)
        for t in (TXT, IMG):
            wait_sent(t, (0,))
            start_both(t, 1)
        for t in (TXT, IMG):
            add_relayed(t, A)
            add_relayed(t, B)
        for t in (TXT, IMG):
            for h in (A, B):
                finish(t, h)
                local_out(t, h).start()
        to_foreign.wait_send()
        for stage in stages:
            for each in stage_copies(*stage):
                each.wait_send()
        for t in (TXT, IMG):
            wait_sent(t, (1, 2))
            for h in (A, B):
                local_out(t, h).wait()

    @pl.when(jnp.logical_not(native))
    def _():
        z_in(TXT, A).start()
        z_in(TXT, A).wait_send()
        z_in(TXT, B).start()
        z_in(TXT, A).wait_recv()
        send_half(TXT, A)
        z_in(TXT, B).wait_send()
        z_in(IMG, A).start()
        z_in(TXT, B).wait_recv()
        send_half(TXT, B)
        z_in(IMG, A).wait_send()
        z_in(IMG, B).start()
        pass_on(TXT, A)
        z_in(IMG, A).wait_recv()
        send_half(IMG, A)
        pass_on(TXT, B)
        from_core(IMG, A)
        from_core(IMG, B)
        other_logits(A)
        z_in(IMG, B).wait_recv()
        send_half(IMG, B)
        other_logits(B)
        from_core(TXT, A)
        from_core(TXT, B)
        pass_on(IMG, A)
        own_logits(A, 0, 2 * tiles)
        same_pairs(A)
        image_terms(A)
        text_early(A)
        text_early(B)
        pass_on(IMG, B)
        reduce(IMG, A, 0).start()
        reduce(IMG, A, 1).start()
        own_logits(B, 0, tiles)
        same_pairs(B)
        text_late(A)
        reduce(TXT, A, 0).start()
        text_late(B)
        reduce(TXT, B, 0).start()
        own_logits(B, tiles, 2 * tiles)
        st_c[0] = own_sums()
        to_native.start()
        image_terms(B)
        add_relayed(IMG, A)
        reduce(IMG, B, 0).start()
        reduce(IMG, B, 1).start()
        wait_sent(TXT, (0,))
        start_both(TXT, 1)
        add_relayed(TXT, A)
        add_relayed(TXT, B)
        finish(IMG, A)
        z_out(IMG, A).start()
        add_relayed(IMG, B)
        wait_sent(TXT, (2,))
        pl.semaphore_signal(turn.at[TXT], inc=1, device_id=sibling, device_id_type=MESH)
        finish(TXT, A)
        z_out(TXT, A).start()
        finish(TXT, B)
        z_out(TXT, B).start()
        wait_sent(IMG, (2,))
        pl.semaphore_signal(turn.at[IMG], inc=1, device_id=sibling, device_id_type=MESH)
        finish(IMG, B)
        z_out(IMG, B).start()
        to_foreign.wait_recv()
        write_totals(st_c[1])
        to_native.wait_send()
        z_in(IMG, B).wait_send()
        wait_sent(TXT, (1,))
        wait_sent(IMG, (0, 1))
        for t in (IMG, TXT):
            for h in (A, B):
                z_out(t, h).wait()

    for t in (TXT, IMG):
        for h in (A, B):
            gather(t, h, 0).wait_send()
            gather(t, h, 1).wait_send()
            across(t, h).wait_send()
            for index in range(SIDE):
                to_core(t, h, index).wait_send()


def per_device(image_embed, text_embed, log_logit_scale, logit_bias):
    rows, width = image_embed.shape
    share = SIDE * rows
    block = share // 2
    pairs = rows * lax.axis_size("blk") * lax.axis_size("dp")
    hbm, vmem = pl.BlockSpec(memory_space=pltpu.HBM), pl.BlockSpec(memory_space=pltpu.VMEM)
    like = jax.ShapeDtypeStruct((2, rows, width), jnp.bfloat16)
    bf16, f32 = jnp.bfloat16, jnp.float32
    gradients, totals = pl.pallas_call(
        functools.partial(kernel, pairs),
        out_shape=(like, jax.ShapeDtypeStruct((8, 128), f32)),
        in_specs=[hbm, hbm, hbm, hbm],
        out_specs=(hbm, vmem),
        scratch_shapes=[
            pltpu.VMEM((2, rows, width), bf16),
            pltpu.VMEM((2, rows, 128), f32),
            pltpu.VMEM((2 * share, width), bf16),
            pltpu.VMEM((2 * share, width), bf16),
            pltpu.VMEM((share, 2 * share), bf16),
            pltpu.VMEM((share, share), bf16),
            pltpu.VMEM((block, TILE), f32),
            pltpu.VMEM((block, TILE), f32),
            pltpu.VMEM((share, width), f32),
            pltpu.VMEM((share, width), f32),
            pltpu.VMEM((2, rows, width), f32),
            pltpu.VMEM((2, rows, width), f32),
            pltpu.VMEM((2, rows // 2, width), f32),
            pltpu.VMEM((2, rows // 2, width), f32),
            pltpu.VMEM((2, rows, width), bf16),
            pltpu.VMEM((3, 8, TILE), f32),
            pltpu.VMEM((4, 24, 128), f32),
            pltpu.VMEM((4, 24, 128), f32),
            pltpu.VMEM((2, 24, 128), f32),
            pltpu.VMEM((4, 24, 128), f32),
            pltpu.VMEM((2, 24, 128), f32),
            pltpu.SMEM((1,), f32),
            pltpu.SMEM((1,), f32),
            pltpu.SemaphoreType.DMA((COPIES,)),
            pltpu.SemaphoreType.DMA((COPIES,)),
            pltpu.SemaphoreType.DMA((8,)),
            pltpu.SemaphoreType.REGULAR((2,)),
        ],
        name="contrastive_step",
        compiler_params=pltpu.CompilerParams(
            collective_id=0, has_side_effects=True, vmem_limit_bytes=62 * 2**20
        ),
    )(log_logit_scale, logit_bias, image_embed, text_embed)
    loss, scale_gradient, bias_gradient = totals[0, :1], totals[1, :1], totals[2, :1]
    return gradients[IMG], gradients[TXT], scale_gradient, bias_gradient, loss


def solution(mesh):
    placed = (P(("blk", "dp"), None), P(("blk", "dp"), None), P(), P())
    return jax.shard_map(
        per_device,
        mesh=mesh,
        in_specs=placed,
        out_specs=(P(("blk", "dp"), None), P(("blk", "dp"), None), P(), P(), P()),
        check_vma=False,
    )
```

```python
import functools

import jax
import jax.numpy as jnp
from jax import lax
from jax.experimental import pallas as pl
from jax.experimental.pallas import tpu as pltpu
from jax.sharding import PartitionSpec as P

EPS = 1e-06
LOG2E = 1.4426950408889634
LN2 = 0.6931471805599453
MESH = pl.DeviceIdType.MESH
SIDE = 4
TILE = 256
TXT, IMG = 0, 1
A, B = 0, 1
OVER_COLS = (((1,), (1,)), ((), ()))
OVER_ROWS = (((0,), (0,)), ((), ()))

Z_IN, GATHER, ACROSS, CORE, REDUCE, Z_OUT = 0, 4, 12, 16, 32, 44
ST_X, ST_Y, ST_C, ST_L, ST_P = 48, 51, 54, 56, 59
COPIES = 60


def kernel(
    pairs, log_scale_ref, bias_ref, img_ref, txt_ref,
    out_grads, out_totals,
    raw, inverses, texts, images, coef_own, coef_other, cos_even, cos_odd,
    grad_txt, grad_img, recv_txt, recv_img, relay_txt, relay_img,
    final, acc, st_x, st_y, st_c, st_l, st_p, send_sem, recv_sem, local_sem, turn,
):
    rows, width = img_ref.shape
    part = rows // 2
    block = SIDE * part
    share = 2 * block
    blk, dp = lax.axis_index("blk"), lax.axis_index("dp")
    zh, x, y = blk // (SIDE * SIDE), (blk // SIDE) % SIDE, blk % SIDE
    zl, core = dp // 2, dp % 2
    native = core == zh

    def device(dx=0, dy=0, dl=0, other_core=False, other_plane=False):
        h = 1 - zh if other_plane else zh
        c = 1 - core if other_core else core
        return {
            "blk": (h * SIDE + (x + dx) % SIDE) * SIDE + (y + dy) % SIDE,
            "dp": ((zl + dl) % SIDE) * 2 + c,
        }

    along_x = [device(dx=d) for d in (1, 2, 3)]
    along_y = [device(dy=d) for d in (1, 2, 3)]
    along_l = [device(dl=d) for d in (1, 2, 3)]
    right = (along_x[0], along_y[0])
    left = (along_x[2], along_y[2])
    sibling = device(other_core=True)
    partner = device(other_core=True, other_plane=True)
    inputs, outputs = (txt_ref, img_ref), (out_grads.at[TXT], out_grads.at[IMG])
    units, grads = (texts, images), (grad_txt, grad_img)
    recvs, relays = (recv_txt, recv_img), (relay_txt, relay_img)

    def copy(number, src, dst, where):
        return pltpu.make_async_remote_copy(
            src_ref=src, dst_ref=dst, send_sem=send_sem.at[number], recv_sem=recv_sem.at[number],
            device_id=where, device_id_type=MESH,
        )

    def half(h):
        return pl.ds(h * part, part)

    def slot(h, index, other=0):
        return pl.ds(other * share + h * block + index * part, part)

    def z_in(t, h):
        return copy(Z_IN + 2 * t + h, inputs[t].at[half(h)], raw.at[t, half(h)], partner)

    def gather(t, h, d):
        return copy(
            GATHER + 4 * t + 2 * h + d, units[t].at[slot(h, 0)], units[t].at[slot(h, (3, 1)[d])], (right, left)[d][t]
        )

    def across(t, h):
        return copy(
            ACROSS + 2 * t + h, units[t].at[slot(h, 0)], units[t].at[slot(h, 2)], (along_x, along_y)[t][1]
        )

    def to_core(t, h, index):
        return copy(
            CORE + 8 * t + 4 * h + index, units[t].at[slot(h, index)], units[t].at[slot(h, index, 1)], sibling
        )

    def reduce(t, h, step):
        onward = step != 1
        to = (right, left)[h if onward else 1 - h][t]
        if step == 0:
            src, dst = slot(h, 2), relays[t].at[h]
        elif step == 1:
            src, dst = slot(h, (3, 1)[h]), recvs[t].at[1 - h, half(h)]
        else:
            src, dst = slot(h, (1, 3)[h]), recvs[t].at[h, half(h)]
        return copy(REDUCE + 6 * t + 3 * h + step, grads[t].at[src], dst, to)

    def z_out(t, h):
        return copy(Z_OUT + 2 * t + h, final.at[t, half(h)], outputs[t].at[half(h)], partner)

    def local_in(t):
        return pltpu.make_async_copy(inputs[t], raw.at[t], local_sem.at[t])

    def local_out(t, h):
        return pltpu.make_async_copy(final.at[t, half(h)], outputs[t].at[half(h)], local_sem.at[2 + 2 * t + h])

    @pl.when(native)
    def _():
        local_in(TXT).start()
        local_in(IMG).start()

    barrier = pltpu.get_barrier_semaphore()
    everyone = along_x + along_y + along_l + [sibling, partner]
    for other in everyone:
        pl.semaphore_signal(barrier, inc=1, device_id=other, device_id_type=MESH)
    pl.semaphore_wait(barrier, len(everyone))

    log_scale = jnp.broadcast_to(log_scale_ref[...], (1, TILE))
    scale = jnp.exp(log_scale)
    scale2 = scale * LOG2E
    bias = jnp.broadcast_to(bias_ref[...], (1, TILE))
    bias2 = bias * LOG2E
    acc[...] = jnp.zeros_like(acc)

    def normalize(t, h):
        for i in range(part // 32):
            at = pl.ds(h * part + i * 32, 32)
            wide = raw[t, at, :].astype(jnp.float32)
            inverse = lax.rsqrt(jnp.sum(wide * wide, axis=1, keepdims=True) + EPS)
            inverses[t, at, :] = jnp.broadcast_to(inverse, (32, 128))
            units[t][pl.ds(h * block + i * 32, 32), :] = (wide * inverse).astype(jnp.bfloat16)

    def send_half(t, h):
        normalize(t, h)
        across(t, h).start()
        gather(t, h, 0).start()
        gather(t, h, 1).start()
        to_core(t, h, 0).start()

    def pass_on(t, h):
        for index, landed in ((3, gather(t, h, 0)), (1, gather(t, h, 1)), (2, across(t, h))):
            landed.wait_recv()
            to_core(t, h, index).start()

    def from_core(t, h):
        for index in range(SIDE):
            to_core(t, h, index).wait_recv()

    def dot_tile(out, first, column):
        out[...] = lax.dot_general(
            images[pl.ds(first, block), :],
            texts[pl.ds(pl.multiple_of(column * TILE, TILE), TILE), :],
            OVER_COLS,
            preferred_element_type=jnp.float32,
        )

    def own_terms(cos_ref, h, column):
        at_cols = pl.ds(pl.multiple_of(column * TILE, TILE), TILE)
        losses = temps = biases = jnp.zeros((8, TILE), jnp.float32)
        strip = 16
        for i in range(block // strip):
            cosine = cos_ref[pl.ds(i * strip, strip), :]
            grown = jnp.exp2(scale2 * cosine + bias2)
            more = 1.0 + grown
            coef = grown / more
            coef_own[pl.ds(h * block + i * strip, strip), at_cols] = coef.astype(jnp.bfloat16)
            fold = (strip // 8, 8, TILE)
            losses += jnp.sum(jnp.log(more).reshape(fold), axis=0)
            temps += jnp.sum((coef * cosine).reshape(fold), axis=0)
            biases += jnp.sum(coef.reshape(fold), axis=0)
        acc[0] += losses
        acc[1] += temps
        acc[2] += biases

    def other_terms(cos_ref, h, column):
        at_cols = pl.ds(pl.multiple_of(column * TILE, TILE), TILE)
        strip = 16
        for i in range(block // strip):
            grown = jnp.exp2(scale2 * cos_ref[pl.ds(i * strip, strip), :] + bias2)
            coef_other[pl.ds(h * block + i * strip, strip), at_cols] = (grown / (1.0 + grown)).astype(jnp.bfloat16)

    def sweep(terms, first, h, start, stop):
        dot_tile(cos_even, first, start)
        count = stop - start

        def body(p, _):
            column = start + 2 * p
            dot_tile(cos_odd, first, column + 1)
            terms(cos_even, h, column)
            dot_tile(cos_even, first, jnp.minimum(column + 2, stop - 1))
            terms(cos_odd, h, column + 1)
            return 0

        lax.fori_loop(0, count // 2, body, 0)
        if count % 2:
            terms(cos_even, h, stop - 1)

    def own_logits(h, start, stop):
        sweep(own_terms, h * block, h, start, stop)

    def other_logits(h):
        sweep(other_terms, share + h * block, h, 0, share // TILE)

    def same_pairs(h):
        lanes = 128
        at_rows, at_cols = pl.ds(h * block, part), pl.ds(h * block, lanes)
        cosine = lax.dot_general(
            images[at_rows, :], texts[at_cols, :], OVER_COLS, preferred_element_type=jnp.float32
        )
        shape = (part, lanes)
        same = lax.broadcasted_iota(jnp.int32, shape, 0) == lax.broadcasted_iota(jnp.int32, shape, 1)
        grown = jnp.exp2(scale2[:, :lanes] * cosine + bias2[:, :lanes])
        more = 1.0 + grown
        inverse = 1.0 / more
        coef = grown * inverse
        coef_own[at_rows, at_cols] = jnp.where(same, -inverse, coef).astype(jnp.bfloat16)
        logit = scale[:, :lanes] * cosine + bias[:, :lanes]
        change = jnp.where(same, -inverse - coef, 0.0)
        fold = (part // 8, 8, lanes)
        acc[0, :, :lanes] += jnp.sum(jnp.where(same, -logit, 0.0).reshape(fold), axis=0)
        acc[1, :, :lanes] += jnp.sum((change * cosine).reshape(fold), axis=0)
        acc[2, :, :lanes] += jnp.sum(change.reshape(fold), axis=0)

    def image_terms(h):
        at_rows = pl.ds(h * block, block)
        grad_img[at_rows, :] = jnp.dot(coef_own[at_rows, :], texts[...], preferred_element_type=jnp.float32)

    def turned_dot(coefs, units_rows):
        return lax.dot_general(coefs, units_rows, OVER_ROWS, preferred_element_type=jnp.float32)

    def text_early(h):
        at_rows = pl.ds(h * block, block)
        grad_txt[at_rows, :] = turned_dot(coef_own[:block, at_rows], images[:block, :]) + turned_dot(
            coef_other[:, at_rows], images[share:, :]
        )

    def text_late(h):
        at_rows = pl.ds(h * block, block)
        grad_txt[at_rows, :] += turned_dot(coef_own[block:, at_rows], images[block:share, :])

    def text_terms(h):
        at_rows = pl.ds(h * block, block)
        grad_txt[at_rows, :] = turned_dot(coef_own[:, at_rows], images[:share, :]) + turned_dot(
            coef_other[:, at_rows], images[share:, :]
        )

    def add_relayed(t, h):
        reduce(t, h, 0).wait_recv()
        grads[t][slot(h, (1, 3)[h]), :] += relays[t][h]
        reduce(t, h, 2).start()

    def finish(t, h):
        reduce(t, h, 1).wait_recv()
        reduce(t, h, 2).wait_recv()
        for i in range(part // 32):
            at = pl.ds(h * part + i * 32, 32)
            inverse = inverses[t, at, :1]
            unit = raw[t, at, :].astype(jnp.float32) * inverse
            scaled = scale[:, :1] * (
                grads[t][pl.ds(h * block + i * 32, 32), :] + recvs[t][0, at, :] + recvs[t][1, at, :]
            )
            along = jnp.sum(unit * scaled, axis=1, keepdims=True)
            final[t, at, :] = ((scaled - unit * along) * inverse).astype(jnp.bfloat16)

    stages = ((ST_X, st_x, x, along_x), (ST_Y, st_y, y, along_y), (ST_L, st_l, zl, along_l), (ST_P, st_p, zh, [partner]))
    to_native = copy(ST_C, st_c.at[0], st_c.at[1], sibling)
    to_foreign = copy(ST_C + 1, st_c.at[0], st_c.at[1], sibling)

    def own_sums():
        return (acc[:, :, :128] + acc[:, :, 128:]).reshape(24, 128)

    def stage_copies(base, buffer, mine, line):
        return [copy(base + i, buffer.at[mine], buffer.at[mine], other) for i, other in enumerate(line)]

    def sums_start(stage, value):
        _, buffer, mine, _ = stages[stage]
        buffer[mine] = value
        for each in stage_copies(*stages[stage]):
            each.start()

    def sums_finish(stage):
        for each in stage_copies(*stages[stage]):
            each.wait_recv()
        buffer, count = stages[stage][1], len(stages[stage][3]) + 1
        return functools.reduce(lambda a, b: a + b, [buffer[i] for i in range(count)])

    def write_totals(totals):
        for k, factor in enumerate((1.0, scale[:, :1], 1.0)):
            total = jnp.sum(jnp.sum(totals[8 * k : 8 * k + 8], axis=0, keepdims=True), axis=1, keepdims=True)
            out_totals[k : k + 1, :] = jnp.broadcast_to(factor * total / pairs, (1, 128))

    tiles = share // TILE

    def wait_sent(t, steps):
        for h in (A, B):
            for step in steps:
                reduce(t, h, step).wait_send()

    def start_both(t, step):
        reduce(t, A, step).start()
        reduce(t, B, step).start()

    def wait_sent(t, steps):
        for step in steps:
            reduce(t, A, step).wait_send()
            reduce(t, B, step).wait_send()

    @pl.when(native)
    def _():
        for t in (TXT, IMG):
            local_in(t).wait()
            send_half(t, A)
            send_half(t, B)
        for t in (TXT, IMG):
            pass_on(t, A)
            pass_on(t, B)
        own_logits(A, 0, tiles)
        own_logits(B, 0, tiles)
        from_core(TXT, A)
        from_core(TXT, B)
        own_logits(A, tiles, 2 * tiles)
        same_pairs(A)
        own_logits(B, tiles, 2 * tiles)
        same_pairs(B)
        image_terms(A)
        image_terms(B)
        from_core(IMG, A)
        other_logits(A)
        to_native.wait_recv()
        sums_start(0, own_sums() + st_c[1])
        from_core(IMG, B)
        other_logits(B)
        sums_start(1, sums_finish(0))
        text_terms(A)
        text_terms(B)
        sums_start(2, sums_finish(1))
        sums_start(3, sums_finish(2))
        totals = sums_finish(3)
        st_c[0] = totals
        to_foreign.start()
        write_totals(totals)
        pl.semaphore_wait(turn.at[IMG], 1)
        start_both(IMG, 0)
        pl.semaphore_wait(turn.at[TXT], 1)
        start_both(TXT, 0)
        wait_sent(IMG, (0,))
        start_both(IMG, 1)
        wait_sent(TXT, (0,))
        start_both(TXT, 1)
        for t in (IMG, TXT):
            add_relayed(t, A)
            add_relayed(t, B)
        for t in (IMG, TXT):
            for h in (A, B):
                finish(t, h)
                local_out(t, h).start()
        to_foreign.wait_send()
        for stage in stages:
            for each in stage_copies(*stage):
                each.wait_send()
        for t in (TXT, IMG):
            wait_sent(t, (1, 2))
            for h in (A, B):
                local_out(t, h).wait()

    @pl.when(jnp.logical_not(native))
    def _():
        z_in(TXT, A).start()
        z_in(TXT, A).wait_send()
        z_in(TXT, B).start()
        z_in(TXT, A).wait_recv()
        send_half(TXT, A)
        z_in(TXT, B).wait_send()
        z_in(IMG, A).start()
        z_in(TXT, B).wait_recv()
        send_half(TXT, B)
        z_in(IMG, A).wait_send()
        z_in(IMG, B).start()
        pass_on(TXT, A)
        z_in(IMG, A).wait_recv()
        send_half(IMG, A)
        pass_on(TXT, B)
        from_core(IMG, A)
        from_core(IMG, B)
        other_logits(A)
        z_in(IMG, B).wait_recv()
        send_half(IMG, B)
        other_logits(B)
        from_core(TXT, A)
        from_core(TXT, B)
        pass_on(IMG, A)
        own_logits(A, 0, 2 * tiles)
        same_pairs(A)
        image_terms(A)
        text_early(A)
        text_early(B)
        pass_on(IMG, B)
        reduce(IMG, A, 0).start()
        reduce(IMG, A, 1).start()
        own_logits(B, 0, tiles)
        same_pairs(B)
        text_late(A)
        reduce(TXT, A, 0).start()
        text_late(B)
        reduce(TXT, B, 0).start()
        own_logits(B, tiles, 2 * tiles)
        st_c[0] = own_sums()
        to_native.start()
        image_terms(B)
        add_relayed(IMG, A)
        reduce(IMG, B, 0).start()
        reduce(IMG, B, 1).start()
        wait_sent(TXT, (0,))
        start_both(TXT, 1)
        add_relayed(TXT, A)
        add_relayed(TXT, B)
        add_relayed(IMG, B)
        pl.semaphore_signal(turn.at[IMG], inc=1, device_id=sibling, device_id_type=MESH)
        finish(IMG, A)
        z_out(IMG, A).start()
        wait_sent(TXT, (2,))
        pl.semaphore_signal(turn.at[TXT], inc=1, device_id=sibling, device_id_type=MESH)
        finish(TXT, A)
        z_out(TXT, A).start()
        finish(TXT, B)
        z_out(TXT, B).start()
        wait_sent(IMG, (2,))
        finish(IMG, B)
        z_out(IMG, B).start()
        to_foreign.wait_recv()
        write_totals(st_c[1])
        to_native.wait_send()
        z_in(IMG, B).wait_send()
        wait_sent(TXT, (1,))
        wait_sent(IMG, (0, 1))
        for t in (IMG, TXT):
            for h in (A, B):
                z_out(t, h).wait()

    for t in (TXT, IMG):
        for h in (A, B):
            gather(t, h, 0).wait_send()
            gather(t, h, 1).wait_send()
            across(t, h).wait_send()
            for index in range(SIDE):
                to_core(t, h, index).wait_send()


def per_device(image_embed, text_embed, log_logit_scale, logit_bias):
    rows, width = image_embed.shape
    share = SIDE * rows
    block = share // 2
    pairs = rows * lax.axis_size("blk") * lax.axis_size("dp")
    hbm, vmem = pl.BlockSpec(memory_space=pltpu.HBM), pl.BlockSpec(memory_space=pltpu.VMEM)
    like = jax.ShapeDtypeStruct((2, rows, width), jnp.bfloat16)
    bf16, f32 = jnp.bfloat16, jnp.float32
    gradients, totals = pl.pallas_call(
        functools.partial(kernel, pairs),
        out_shape=(like, jax.ShapeDtypeStruct((8, 128), f32)),
        in_specs=[vmem, vmem, hbm, hbm],
        out_specs=(hbm, vmem),
        scratch_shapes=[
            pltpu.VMEM((2, rows, width), bf16),
            pltpu.VMEM((2, rows, 128), f32),
            pltpu.VMEM((2 * share, width), bf16),
            pltpu.VMEM((2 * share, width), bf16),
            pltpu.VMEM((share, 2 * share), bf16),
            pltpu.VMEM((share, share), bf16),
            pltpu.VMEM((block, TILE), f32),
            pltpu.VMEM((block, TILE), f32),
            pltpu.VMEM((share, width), f32),
            pltpu.VMEM((share, width), f32),
            pltpu.VMEM((2, rows, width), f32),
            pltpu.VMEM((2, rows, width), f32),
            pltpu.VMEM((2, rows // 2, width), f32),
            pltpu.VMEM((2, rows // 2, width), f32),
            pltpu.VMEM((2, rows, width), bf16),
            pltpu.VMEM((3, 8, TILE), f32),
            pltpu.VMEM((4, 24, 128), f32),
            pltpu.VMEM((4, 24, 128), f32),
            pltpu.VMEM((2, 24, 128), f32),
            pltpu.VMEM((4, 24, 128), f32),
            pltpu.VMEM((2, 24, 128), f32),
            pltpu.SemaphoreType.DMA((COPIES,)),
            pltpu.SemaphoreType.DMA((COPIES,)),
            pltpu.SemaphoreType.DMA((6,)),
            pltpu.SemaphoreType.REGULAR((2,)),
        ],
        name="contrastive_step",
        compiler_params=pltpu.CompilerParams(
            collective_id=0, has_side_effects=True, vmem_limit_bytes=62 * 2**20
        ),
    )(log_logit_scale.reshape(1, 1), logit_bias.reshape(1, 1), image_embed, text_embed)
    loss, scale_gradient, bias_gradient = totals[0, :1], totals[1, :1], totals[2, :1]
    return gradients[IMG], gradients[TXT], scale_gradient, bias_gradient, loss


def solution(mesh):
    placed = (P(("blk", "dp"), None), P(("blk", "dp"), None), P(), P())
    return jax.shard_map(
        per_device,
        mesh=mesh,
        in_specs=placed,
        out_specs=(P(("blk", "dp"), None), P(("blk", "dp"), None), P(), P(), P()),
        check_vma=False,
    )
```

```python
import functools

import jax
import jax.numpy as jnp
from jax import lax
from jax.experimental import pallas as pl
from jax.experimental.pallas import tpu as pltpu
from jax.sharding import PartitionSpec as P

EPS = 1e-06
LOG2E = 1.4426950408889634
LN2 = 0.6931471805599453
MESH = pl.DeviceIdType.MESH
SIDE = 4
TILE = 256
TXT, IMG = 0, 1
A, B = 0, 1
OVER_COLS = (((1,), (1,)), ((), ()))
OVER_ROWS = (((0,), (0,)), ((), ()))

Z_IN, GATHER, ACROSS, CORE, REDUCE, Z_OUT = 0, 4, 12, 16, 32, 44
ST_X, ST_Y, ST_C, ST_L, ST_P = 48, 51, 54, 56, 59
COPIES = 60


def kernel(
    pairs, log_scale_ref, bias_ref, img_ref, txt_ref,
    out_grads, out_totals,
    raw, inverses, texts, images, coef_own, coef_other, cos_even, cos_odd,
    grad_txt, grad_img, recv_txt, recv_img, relay_txt, relay_img,
    final, acc, st_x, st_y, st_c, st_l, st_p, send_sem, recv_sem, local_sem, turn,
):
    rows, width = img_ref.shape
    part = rows // 2
    block = SIDE * part
    share = 2 * block
    blk, dp = lax.axis_index("blk"), lax.axis_index("dp")
    zh, x, y = blk // (SIDE * SIDE), (blk // SIDE) % SIDE, blk % SIDE
    zl, core = dp // 2, dp % 2
    native = core == zh

    def device(dx=0, dy=0, dl=0, other_core=False, other_plane=False):
        h = 1 - zh if other_plane else zh
        c = 1 - core if other_core else core
        return {
            "blk": (h * SIDE + (x + dx) % SIDE) * SIDE + (y + dy) % SIDE,
            "dp": ((zl + dl) % SIDE) * 2 + c,
        }

    along_x = [device(dx=d) for d in (1, 2, 3)]
    along_y = [device(dy=d) for d in (1, 2, 3)]
    along_l = [device(dl=d) for d in (1, 2, 3)]
    right = (along_x[0], along_y[0])
    left = (along_x[2], along_y[2])
    sibling = device(other_core=True)
    partner = device(other_core=True, other_plane=True)
    inputs, outputs = (txt_ref, img_ref), (out_grads.at[TXT], out_grads.at[IMG])
    units, grads = (texts, images), (grad_txt, grad_img)
    recvs, relays = (recv_txt, recv_img), (relay_txt, relay_img)

    def copy(number, src, dst, where):
        return pltpu.make_async_remote_copy(
            src_ref=src, dst_ref=dst, send_sem=send_sem.at[number], recv_sem=recv_sem.at[number],
            device_id=where, device_id_type=MESH,
        )

    def half(h):
        return pl.ds(h * part, part)

    def slot(h, index, other=0):
        return pl.ds(other * share + h * block + index * part, part)

    def z_in(t, h):
        return copy(Z_IN + 2 * t + h, inputs[t].at[half(h)], raw.at[t, half(h)], partner)

    def gather(t, h, d):
        return copy(
            GATHER + 4 * t + 2 * h + d, units[t].at[slot(h, 0)], units[t].at[slot(h, (3, 1)[d])], (right, left)[d][t]
        )

    def across(t, h):
        return copy(
            ACROSS + 2 * t + h, units[t].at[slot(h, 0)], units[t].at[slot(h, 2)], (along_x, along_y)[t][1]
        )

    def to_core(t, h, index):
        return copy(
            CORE + 8 * t + 4 * h + index, units[t].at[slot(h, index)], units[t].at[slot(h, index, 1)], sibling
        )

    def reduce(t, h, step):
        onward = step != 1
        to = (right, left)[h if onward else 1 - h][t]
        if step == 0:
            src, dst = slot(h, 2), relays[t].at[h]
        elif step == 1:
            src, dst = slot(h, (3, 1)[h]), recvs[t].at[1 - h, half(h)]
        else:
            src, dst = slot(h, (1, 3)[h]), recvs[t].at[h, half(h)]
        return copy(REDUCE + 6 * t + 3 * h + step, grads[t].at[src], dst, to)

    def z_out(t, h):
        return copy(Z_OUT + 2 * t + h, final.at[t, half(h)], outputs[t].at[half(h)], partner)

    def local_in(t):
        return pltpu.make_async_copy(inputs[t], raw.at[t], local_sem.at[t])

    def local_out(t, h):
        return pltpu.make_async_copy(final.at[t, half(h)], outputs[t].at[half(h)], local_sem.at[2 + 2 * t + h])

    @pl.when(native)
    def _():
        local_in(TXT).start()
        local_in(IMG).start()

    barrier = pltpu.get_barrier_semaphore()
    everyone = [partner] + along_l + along_x + along_y + [sibling]
    for other in everyone:
        pl.semaphore_signal(barrier, inc=1, device_id=other, device_id_type=MESH)

    log_scale = jnp.broadcast_to(log_scale_ref[...], (1, TILE))
    scale = jnp.exp(log_scale)
    scale2 = scale * LOG2E
    bias = jnp.broadcast_to(bias_ref[...], (1, TILE))
    bias2 = bias * LOG2E
    acc[...] = jnp.zeros_like(acc)
    pl.semaphore_wait(barrier, len(everyone))

    def normalize(t, h):
        for i in range(part // 32):
            at = pl.ds(h * part + i * 32, 32)
            wide = raw[t, at, :].astype(jnp.float32)
            inverse = lax.rsqrt(jnp.sum(wide * wide, axis=1, keepdims=True) + EPS)
            inverses[t, at, :] = jnp.broadcast_to(inverse, (32, 128))
            units[t][pl.ds(h * block + i * 32, 32), :] = (wide * inverse).astype(jnp.bfloat16)

    def send_half(t, h):
        normalize(t, h)
        across(t, h).start()
        gather(t, h, 0).start()
        gather(t, h, 1).start()
        to_core(t, h, 0).start()

    def pass_on(t, h):
        for index, landed in ((3, gather(t, h, 0)), (1, gather(t, h, 1)), (2, across(t, h))):
            landed.wait_recv()
            to_core(t, h, index).start()

    def from_core(t, h):
        for index in range(SIDE):
            to_core(t, h, index).wait_recv()

    def dot_tile(out, first, column):
        out[...] = lax.dot_general(
            images[pl.ds(first, block), :],
            texts[pl.ds(pl.multiple_of(column * TILE, TILE), TILE), :],
            OVER_COLS,
            preferred_element_type=jnp.float32,
        )

    def own_terms(cos_ref, h, column):
        at_cols = pl.ds(pl.multiple_of(column * TILE, TILE), TILE)
        losses = temps = biases = jnp.zeros((8, TILE), jnp.float32)
        strip = 16
        for i in range(block // strip):
            cosine = cos_ref[pl.ds(i * strip, strip), :]
            grown = jnp.exp2(scale2 * cosine + bias2)
            more = 1.0 + grown
            coef = grown / more
            coef_own[pl.ds(h * block + i * strip, strip), at_cols] = coef.astype(jnp.bfloat16)
            fold = (strip // 8, 8, TILE)
            losses += jnp.sum(jnp.log(more).reshape(fold), axis=0)
            temps += jnp.sum((coef * cosine).reshape(fold), axis=0)
            biases += jnp.sum(coef.reshape(fold), axis=0)
        acc[0] += losses
        acc[1] += temps
        acc[2] += biases

    def other_terms(cos_ref, h, column):
        at_cols = pl.ds(pl.multiple_of(column * TILE, TILE), TILE)
        strip = 16
        for i in range(block // strip):
            grown = jnp.exp2(scale2 * cos_ref[pl.ds(i * strip, strip), :] + bias2)
            coef_other[pl.ds(h * block + i * strip, strip), at_cols] = (grown / (1.0 + grown)).astype(jnp.bfloat16)

    def sweep(terms, first, h, start, stop):
        dot_tile(cos_even, first, start)
        count = stop - start

        def body(p, _):
            column = start + 2 * p
            dot_tile(cos_odd, first, column + 1)
            terms(cos_even, h, column)
            dot_tile(cos_even, first, jnp.minimum(column + 2, stop - 1))
            terms(cos_odd, h, column + 1)
            return 0

        lax.fori_loop(0, count // 2, body, 0)
        if count % 2:
            terms(cos_even, h, stop - 1)

    def own_logits(h, start, stop):
        sweep(own_terms, h * block, h, start, stop)

    def other_logits(h):
        sweep(other_terms, share + h * block, h, 0, share // TILE)

    def same_pairs(h):
        lanes = 128
        at_rows, at_cols = pl.ds(h * block, part), pl.ds(h * block, lanes)
        cosine = lax.dot_general(
            images[at_rows, :], texts[at_cols, :], OVER_COLS, preferred_element_type=jnp.float32
        )
        shape = (part, lanes)
        same = lax.broadcasted_iota(jnp.int32, shape, 0) == lax.broadcasted_iota(jnp.int32, shape, 1)
        grown = jnp.exp2(scale2[:, :lanes] * cosine + bias2[:, :lanes])
        more = 1.0 + grown
        inverse = 1.0 / more
        coef = grown * inverse
        coef_own[at_rows, at_cols] = jnp.where(same, -inverse, coef).astype(jnp.bfloat16)
        logit = scale[:, :lanes] * cosine + bias[:, :lanes]
        change = jnp.where(same, -inverse - coef, 0.0)
        fold = (part // 8, 8, lanes)
        acc[0, :, :lanes] += jnp.sum(jnp.where(same, -logit, 0.0).reshape(fold), axis=0)
        acc[1, :, :lanes] += jnp.sum((change * cosine).reshape(fold), axis=0)
        acc[2, :, :lanes] += jnp.sum(change.reshape(fold), axis=0)

    def image_terms(h):
        at_rows = pl.ds(h * block, block)
        grad_img[at_rows, :] = jnp.dot(coef_own[at_rows, :], texts[...], preferred_element_type=jnp.float32)

    def turned_dot(coefs, units_rows):
        return lax.dot_general(coefs, units_rows, OVER_ROWS, preferred_element_type=jnp.float32)

    def text_early(h):
        at_rows = pl.ds(h * block, block)
        grad_txt[at_rows, :] = turned_dot(coef_own[:block, at_rows], images[:block, :]) + turned_dot(
            coef_other[:, at_rows], images[share:, :]
        )

    def text_late(h):
        at_rows = pl.ds(h * block, block)
        grad_txt[at_rows, :] += turned_dot(coef_own[block:, at_rows], images[block:share, :])

    def text_terms(h):
        at_rows = pl.ds(h * block, block)
        grad_txt[at_rows, :] = turned_dot(coef_own[:, at_rows], images[:share, :]) + turned_dot(
            coef_other[:, at_rows], images[share:, :]
        )

    def add_relayed(t, h):
        reduce(t, h, 0).wait_recv()
        grads[t][slot(h, (1, 3)[h]), :] += relays[t][h]
        reduce(t, h, 2).start()

    def finish(t, h):
        reduce(t, h, 1).wait_recv()
        reduce(t, h, 2).wait_recv()
        for i in range(part // 32):
            at = pl.ds(h * part + i * 32, 32)
            inverse = inverses[t, at, :1]
            unit = raw[t, at, :].astype(jnp.float32) * inverse
            scaled = scale[:, :1] * (
                grads[t][pl.ds(h * block + i * 32, 32), :] + recvs[t][0, at, :] + recvs[t][1, at, :]
            )
            along = jnp.sum(unit * scaled, axis=1, keepdims=True)
            final[t, at, :] = ((scaled - unit * along) * inverse).astype(jnp.bfloat16)

    stages = ((ST_X, st_x, x, along_x), (ST_Y, st_y, y, along_y), (ST_L, st_l, zl, along_l), (ST_P, st_p, zh, [partner]))
    to_native = copy(ST_C, st_c.at[0], st_c.at[1], sibling)
    to_foreign = copy(ST_C + 1, st_c.at[0], st_c.at[1], sibling)

    def own_sums():
        return (acc[:, :, :128] + acc[:, :, 128:]).reshape(24, 128)

    def stage_copies(base, buffer, mine, line):
        return [copy(base + i, buffer.at[mine], buffer.at[mine], other) for i, other in enumerate(line)]

    def sums_start(stage, value):
        _, buffer, mine, _ = stages[stage]
        buffer[mine] = value
        for each in stage_copies(*stages[stage]):
            each.start()

    def sums_finish(stage):
        for each in stage_copies(*stages[stage]):
            each.wait_recv()
        buffer, count = stages[stage][1], len(stages[stage][3]) + 1
        return functools.reduce(lambda a, b: a + b, [buffer[i] for i in range(count)])

    def write_totals(totals):
        for k, factor in enumerate((1.0, scale[:, :1], 1.0)):
            total = jnp.sum(jnp.sum(totals[8 * k : 8 * k + 8], axis=0, keepdims=True), axis=1, keepdims=True)
            out_totals[k : k + 1, :] = jnp.broadcast_to(factor * total / pairs, (1, 128))

    tiles = share // TILE

    def wait_sent(t, steps):
        for h in (A, B):
            for step in steps:
                reduce(t, h, step).wait_send()

    def start_both(t, step):
        reduce(t, A, step).start()
        reduce(t, B, step).start()

    def wait_sent(t, steps):
        for step in steps:
            reduce(t, A, step).wait_send()
            reduce(t, B, step).wait_send()

    @pl.when(native)
    def _():
        for t in (TXT, IMG):
            local_in(t).wait()
            send_half(t, A)
            send_half(t, B)
        for t in (TXT, IMG):
            pass_on(t, A)
            pass_on(t, B)
        own_logits(A, 0, tiles)
        own_logits(B, 0, tiles)
        from_core(TXT, A)
        from_core(TXT, B)
        own_logits(A, tiles, 2 * tiles)
        same_pairs(A)
        own_logits(B, tiles, 2 * tiles)
        same_pairs(B)
        image_terms(A)
        image_terms(B)
        from_core(IMG, A)
        other_logits(A)
        to_native.wait_recv()
        sums_start(0, own_sums() + st_c[1])
        from_core(IMG, B)
        other_logits(B)
        sums_start(1, sums_finish(0))
        text_terms(A)
        text_terms(B)
        sums_start(2, sums_finish(1))
        sums_start(3, sums_finish(2))
        totals = sums_finish(3)
        st_c[0] = totals
        to_foreign.start()
        write_totals(totals)
        pl.semaphore_wait(turn.at[IMG], 1)
        start_both(IMG, 0)
        pl.semaphore_wait(turn.at[TXT], 1)
        start_both(TXT, 0)
        wait_sent(IMG, (0,))
        start_both(IMG, 1)
        wait_sent(TXT, (0,))
        start_both(TXT, 1)
        for t in (IMG, TXT):
            add_relayed(t, A)
            add_relayed(t, B)
        for t in (IMG, TXT):
            for h in (A, B):
                finish(t, h)
                local_out(t, h).start()
        to_foreign.wait_send()
        for stage in stages:
            for each in stage_copies(*stage):
                each.wait_send()
        for t in (TXT, IMG):
            wait_sent(t, (1, 2))
            for h in (A, B):
                local_out(t, h).wait()

    @pl.when(jnp.logical_not(native))
    def _():
        z_in(TXT, A).start()
        z_in(TXT, A).wait_send()
        z_in(TXT, B).start()
        z_in(TXT, A).wait_recv()
        send_half(TXT, A)
        z_in(TXT, B).wait_send()
        z_in(IMG, A).start()
        z_in(TXT, B).wait_recv()
        send_half(TXT, B)
        z_in(IMG, A).wait_send()
        z_in(IMG, B).start()
        pass_on(TXT, A)
        z_in(IMG, A).wait_recv()
        send_half(IMG, A)
        pass_on(TXT, B)
        from_core(IMG, A)
        from_core(IMG, B)
        other_logits(A)
        z_in(IMG, B).wait_recv()
        send_half(IMG, B)
        other_logits(B)
        from_core(TXT, A)
        from_core(TXT, B)
        pass_on(IMG, A)
        own_logits(A, 0, 2 * tiles)
        same_pairs(A)
        image_terms(A)
        text_early(A)
        text_early(B)
        pass_on(IMG, B)
        reduce(IMG, A, 0).start()
        reduce(IMG, A, 1).start()
        own_logits(B, 0, tiles)
        same_pairs(B)
        text_late(A)
        reduce(TXT, A, 0).start()
        text_late(B)
        reduce(TXT, B, 0).start()
        own_logits(B, tiles, 2 * tiles)
        st_c[0] = own_sums()
        to_native.start()
        image_terms(B)
        add_relayed(IMG, A)
        reduce(IMG, B, 0).start()
        reduce(IMG, B, 1).start()
        wait_sent(TXT, (0,))
        start_both(TXT, 1)
        add_relayed(TXT, A)
        add_relayed(TXT, B)
        add_relayed(IMG, B)
        pl.semaphore_signal(turn.at[IMG], inc=1, device_id=sibling, device_id_type=MESH)
        finish(IMG, A)
        z_out(IMG, A).start()
        wait_sent(TXT, (2,))
        pl.semaphore_signal(turn.at[TXT], inc=1, device_id=sibling, device_id_type=MESH)
        finish(TXT, A)
        z_out(TXT, A).start()
        finish(TXT, B)
        z_out(TXT, B).start()
        wait_sent(IMG, (2,))
        finish(IMG, B)
        z_out(IMG, B).start()
        to_foreign.wait_recv()
        write_totals(st_c[1])
        to_native.wait_send()
        z_in(IMG, B).wait_send()
        wait_sent(TXT, (1,))
        wait_sent(IMG, (0, 1))
        for t in (IMG, TXT):
            for h in (A, B):
                z_out(t, h).wait()

    for t in (TXT, IMG):
        for h in (A, B):
            gather(t, h, 0).wait_send()
            gather(t, h, 1).wait_send()
            across(t, h).wait_send()
            for index in range(SIDE):
                to_core(t, h, index).wait_send()


def per_device(image_embed, text_embed, log_logit_scale, logit_bias):
    rows, width = image_embed.shape
    share = SIDE * rows
    block = share // 2
    pairs = rows * lax.axis_size("blk") * lax.axis_size("dp")
    hbm, vmem = pl.BlockSpec(memory_space=pltpu.HBM), pl.BlockSpec(memory_space=pltpu.VMEM)
    like = jax.ShapeDtypeStruct((2, rows, width), jnp.bfloat16)
    bf16, f32 = jnp.bfloat16, jnp.float32
    gradients, totals = pl.pallas_call(
        functools.partial(kernel, pairs),
        out_shape=(like, jax.ShapeDtypeStruct((8, 128), f32)),
        in_specs=[vmem, vmem, hbm, hbm],
        out_specs=(hbm, vmem),
        scratch_shapes=[
            pltpu.VMEM((2, rows, width), bf16),
            pltpu.VMEM((2, rows, 128), f32),
            pltpu.VMEM((2 * share, width), bf16),
            pltpu.VMEM((2 * share, width), bf16),
            pltpu.VMEM((share, 2 * share), bf16),
            pltpu.VMEM((share, share), bf16),
            pltpu.VMEM((block, TILE), f32),
            pltpu.VMEM((block, TILE), f32),
            pltpu.VMEM((share, width), f32),
            pltpu.VMEM((share, width), f32),
            pltpu.VMEM((2, rows, width), f32),
            pltpu.VMEM((2, rows, width), f32),
            pltpu.VMEM((2, rows // 2, width), f32),
            pltpu.VMEM((2, rows // 2, width), f32),
            pltpu.VMEM((2, rows, width), bf16),
            pltpu.VMEM((3, 8, TILE), f32),
            pltpu.VMEM((4, 24, 128), f32),
            pltpu.VMEM((4, 24, 128), f32),
            pltpu.VMEM((2, 24, 128), f32),
            pltpu.VMEM((4, 24, 128), f32),
            pltpu.VMEM((2, 24, 128), f32),
            pltpu.SemaphoreType.DMA((COPIES,)),
            pltpu.SemaphoreType.DMA((COPIES,)),
            pltpu.SemaphoreType.DMA((6,)),
            pltpu.SemaphoreType.REGULAR((2,)),
        ],
        name="contrastive_step",
        compiler_params=pltpu.CompilerParams(
            collective_id=0, has_side_effects=True, vmem_limit_bytes=62 * 2**20
        ),
    )(log_logit_scale.reshape(1, 1), logit_bias.reshape(1, 1), image_embed, text_embed)
    loss, scale_gradient, bias_gradient = totals[0, :1], totals[1, :1], totals[2, :1]
    return gradients[IMG], gradients[TXT], scale_gradient, bias_gradient, loss


def solution(mesh):
    placed = (P(("blk", "dp"), None), P(("blk", "dp"), None), P(), P())
    return jax.shard_map(
        per_device,
        mesh=mesh,
        in_specs=placed,
        out_specs=(P(("blk", "dp"), None), P(("blk", "dp"), None), P(), P(), P()),
        check_vma=False,
    )
```
